32 devices in a mesh: grp: 1, gx: 32 (over z, y, x, core).
Axes of the slice: x: 2, y: 2, z: 4, core: 2. Of those that a mesh axis runs over, the one named last changes fastest.
Arguments:
- field: bfloat16 [256, 32, 2, 32, 256], P(('grp', 'gx')), may hold values from -6 to 6
- cotangent: bfloat16 [256, 32, 2, 32, 256], P(('grp', 'gx')), may hold values from -6 to 6
- spectral_weight: bfloat16 [2, 32, 32, 768, 24], P(None, None, None, 'gx'), may hold values from -4 to 4
- local_weight: bfloat16 [32, 32], replicated, may hold values from -1 to 1
Outputs:
- output: bfloat16 [256, 32, 2, 32, 256], P(('grp', 'gx'))
- grad_field: bfloat16 [256, 32, 2, 32, 256], P(('grp', 'gx'))
- grad_spectral: float32 [2, 32, 32, 768, 24], P(None, None, None, ('grp', 'gx'))
- grad_local: float32 [32, 32], P('grp')
The draws below stay inside these ranges and needn't reach their ends.
All inputs are finite; a program needn't handle non-finite values.
Results may differ from the reference program's by a relative error of at most 0.0065.
Values sent between devices are 32-bit elements; how exact they have to be, the bound alone decides.
No kernel may reach another device: no remote copies, remote signals or barrier semaphores. Data moves between devices by JAX's collectives and lax.ppermute only.
A program may use at most 256 MiB of HBM per device.

```python
import math
import jax
import jax.numpy as jnp
from jax import lax

NX = 256
NY = 256
C = 32
KX = 24
KY = 24
PAIRS = 32


def block_levels(own_key, shape, pieces, smallest, largest):
    gain = 1.0
    for dim, parts in pieces:
        steps = jax.random.uniform(jax.random.fold_in(jax.random.fold_in(own_key, 6), dim), (parts,), jnp.float32, smallest / len(pieces), largest / len(pieces))
        gain = gain * jnp.repeat(jnp.exp(steps), shape[dim] // parts).reshape((-1,) + (1,) * (len(shape) - 1 - dim))
    return gain


def scatter_about(stream_key, extent, deviation, reach, cuts=(), held_as=jnp.bfloat16):
    array = deviation * jax.random.normal(stream_key, extent, jnp.float32)
    if cuts:
        array = array * block_levels(stream_key, extent, cuts, -0.22, 0.18)
    return jnp.clip(array, -reach, reach).astype(held_as)


def setup_inputs(seed: int = 0, part: int = 0) -> dict:
    streams_of = jax.random.split(jax.random.key(seed), 5)
    part_keys = jax.random.split(jax.random.fold_in(streams_of[4], part), 5)
    field = scatter_about(part_keys[0], (NX, PAIRS, 2, C, NY), 1.0, 6.0, ((0, 32),))
    cotangent = scatter_about(part_keys[1], (NX, PAIRS, 2, C, NY), 1.0, 6.0, ((0, 32),))
    spectral_weight = scatter_about(streams_of[2], (2, C, C, KY * PAIRS, KX), 2 ** -0.5, 4.0, ((3, 32),))
    local_weight = scatter_about(streams_of[3], (C, C), C ** -0.5, 1.0)
    return dict(field=field, cotangent=cotangent, spectral_weight=spectral_weight, local_weight=local_weight)


def phases(length, kept):
    rows_idx = jnp.arange(length, dtype=jnp.int32)[:, None]
    cols_idx = jnp.arange(kept, dtype=jnp.int32)[None, :]
    freqs = jnp.where(cols_idx < kept // 2, cols_idx, cols_idx - kept)
    angles = (rows_idx * freqs % length).astype(jnp.float32) * (2.0 * math.pi / length)
    factor = 1.0 / math.sqrt(length)
    return (jnp.cos(angles) * factor, -jnp.sin(angles) * factor)

def spectral_rows(source, cosines, sines):
    real_part = source[:, :, 0].astype(jnp.float32)
    imag_part = source[:, :, 1].astype(jnp.float32)
    cosines = cosines.astype(jnp.float32)
    sines = sines.astype(jnp.float32)

    def product(operand, matrix):
        return jnp.einsum('xpcn,nk->ckpx', operand, matrix, precision=lax.Precision.HIGHEST)
    out_re = product(real_part, cosines) - product(imag_part, sines)
    out_im = product(real_part, sines) + product(imag_part, cosines)
    stacked = jnp.stack([out_re, out_im])
    return stacked.reshape(2, stacked.shape[1], stacked.shape[2] * stacked.shape[3], stacked.shape[4])

def modes_x(block, cosines, sines):

    def product(operand, matrix):
        return jnp.einsum('cmn,nk->cmk', operand, matrix, precision=lax.Precision.HIGHEST)
    out_re = product(block[0], cosines) - product(block[1], sines)
    out_im = product(block[0], sines) + product(block[1], cosines)
    return jnp.stack([out_re, out_im]).astype(jnp.bfloat16)

def spectral_mix(coeffs, grads, weights):
    coeffs = coeffs.astype(jnp.float32)
    grads = grads.astype(jnp.float32)
    weights = weights.astype(jnp.float32)

    def product(form, left_op, right_op):
        return jnp.einsum(form, left_op, right_op, precision=lax.Precision.HIGHEST)
    forward_form = 'cmk,cdmk->dmk'
    adjoint_form = 'dmk,cdmk->cmk'
    outer_form = 'cmk,dmk->cdmk'
    mixed_re = product(forward_form, coeffs[0], weights[0]) - product(forward_form, coeffs[1], weights[1])
    mixed_im = product(forward_form, coeffs[0], weights[1]) + product(forward_form, coeffs[1], weights[0])
    back_re = product(adjoint_form, grads[0], weights[0]) + product(adjoint_form, grads[1], weights[1])
    back_im = product(adjoint_form, grads[1], weights[0]) - product(adjoint_form, grads[0], weights[1])
    grad_re = product(outer_form, coeffs[0], grads[0]) + product(outer_form, coeffs[1], grads[1])
    grad_im = product(outer_form, coeffs[0], grads[1]) - product(outer_form, coeffs[1], grads[0])
    mixed = jnp.stack([mixed_re, mixed_im]).astype(jnp.bfloat16)
    back = jnp.stack([back_re, back_im]).astype(jnp.bfloat16)
    return (mixed, back, jnp.stack([grad_re, grad_im]))

def spatial_x(coeffs, cosines, sines):
    real_part = coeffs[0].astype(jnp.float32)
    imag_part = coeffs[1].astype(jnp.float32)

    def product(operand, matrix):
        return jnp.einsum('cmk,nk->cmn', operand, matrix, precision=lax.Precision.HIGHEST)
    out_re = product(real_part, cosines) + product(imag_part, sines)
    out_im = product(imag_part, cosines) - product(real_part, sines)
    return jnp.stack([out_re, out_im])

def spatial_y(block, cosines, sines, kept):
    shaped = block.reshape(2, block.shape[1], kept, block.shape[2] // kept, block.shape[3])

    def product(operand, matrix):
        return jnp.einsum('ckpx,nk->xpcn', operand, matrix, precision=lax.Precision.HIGHEST)
    out_re = product(shaped[0], cosines) + product(shaped[1], sines)
    out_im = product(shaped[1], cosines) - product(shaped[0], sines)
    return jnp.stack([out_re, out_im], axis=2)

def reference(field, cotangent, spectral_weight, local_weight):
    cosines_y, sines_y = phases(NY, KY)
    low_cosines = cosines_y.astype(jnp.bfloat16)
    low_sines = sines_y.astype(jnp.bfloat16)
    field_cols = spectral_rows(field, low_cosines, low_sines)
    cot_cols = spectral_rows(cotangent, low_cosines, low_sines)
    cosines_x, sines_x = phases(NX, KX)
    field_hat = modes_x(field_cols, cosines_x, sines_x)
    cot_hat = modes_x(cot_cols, cosines_x, sines_x)
    mixed, back, grad_spectral = spectral_mix(field_hat, cot_hat, spectral_weight)
    mixed_cols = spatial_x(mixed, cosines_x, sines_x)
    back_cols = spatial_x(back, cosines_x, sines_x)
    field_f = field.astype(jnp.float32)
    cot_f = cotangent.astype(jnp.float32)
    local_f = local_weight.astype(jnp.float32)
    local_term = jnp.einsum('xprcn,cd->xprdn', field_f, local_f, precision=lax.Precision.HIGHEST)
    output = (spatial_y(mixed_cols, cosines_y, sines_y, KY) + local_term).astype(jnp.bfloat16)
    local_back = jnp.einsum('xprdn,cd->xprcn', cot_f, local_f, precision=lax.Precision.HIGHEST)
    grad_field = (spatial_y(back_cols, cosines_y, sines_y, KY) + local_back).astype(jnp.bfloat16)
    norm_factor = 1.0 / math.sqrt(NX * NY * PAIRS * 2.0)
    grad_local = jnp.einsum('xprcn,xprdn->cd', field_f, cot_f, precision=lax.Precision.HIGHEST) * norm_factor
    return (output, grad_field, grad_spectral, grad_local)
```

```python
import functools
import math

import numpy as np

import jax
import jax.numpy as jnp
from jax import lax
from jax.experimental import pallas as pl
from jax.experimental.pallas import tpu as pltpu
from jax.sharding import PartitionSpec as P

NX = 256
NY = 256
KY = 24
PAIRS = 32

F32 = jnp.float32
BF16 = jnp.bfloat16


def phases(length, kept):
    rows_idx = jnp.arange(length, dtype=jnp.int32)[:, None]
    cols_idx = jnp.arange(kept, dtype=jnp.int32)[None, :]
    freqs = jnp.where(cols_idx < kept // 2, cols_idx, cols_idx - kept)
    angles = (rows_idx * freqs % length).astype(jnp.float32) * (2.0 * math.pi / length)
    factor = 1.0 / math.sqrt(length)
    return (jnp.cos(angles) * factor, -jnp.sin(angles) * factor)


def spectral_rows(source, cosines, sines):
    real_part = source[:, :, 0]
    imag_part = source[:, :, 1]

    def product(operand, matrix):
        return jnp.einsum("xpcn,nk->xckp", operand, matrix, preferred_element_type=jnp.float32)

    out_re = product(real_part, cosines) - product(imag_part, sines)
    out_im = product(real_part, sines) + product(imag_part, cosines)
    stacked = jnp.stack([out_re, out_im], axis=1)
    return stacked.reshape(
        stacked.shape[0], 2, stacked.shape[2], stacked.shape[3] * stacked.shape[4]
    )


def modes_x(block, cosines, sines):

    def product(operand, matrix):
        return jnp.einsum("ncm,nk->cmk", operand, matrix, precision=lax.Precision.HIGHEST)

    out_re = product(block[:, 0], cosines) - product(block[:, 1], sines)
    out_im = product(block[:, 0], sines) + product(block[:, 1], cosines)
    return jnp.stack([out_re, out_im]).astype(jnp.bfloat16)


def spectral_mix(coeffs, grads, weights):

    def product(form, left_op, right_op):
        return jnp.einsum(form, left_op, right_op, preferred_element_type=jnp.float32)

    forward_form = "cmk,cdmk->dmk"
    adjoint_form = "dmk,cdmk->cmk"
    outer_form = "cmk,dmk->cdmk"
    mixed_re = product(forward_form, coeffs[0], weights[0]) - product(
        forward_form, coeffs[1], weights[1]
    )
    mixed_im = product(forward_form, coeffs[0], weights[1]) + product(
        forward_form, coeffs[1], weights[0]
    )
    back_re = product(adjoint_form, grads[0], weights[0]) + product(
        adjoint_form, grads[1], weights[1]
    )
    back_im = product(adjoint_form, grads[1], weights[0]) - product(
        adjoint_form, grads[0], weights[1]
    )
    grad_re = product(outer_form, coeffs[0], grads[0]) + product(outer_form, coeffs[1], grads[1])
    grad_im = product(outer_form, coeffs[0], grads[1]) - product(outer_form, coeffs[1], grads[0])
    mixed = jnp.stack([mixed_re, mixed_im]).astype(jnp.bfloat16)
    back = jnp.stack([back_re, back_im]).astype(jnp.bfloat16)
    return (mixed, back, jnp.stack([grad_re, grad_im]))


def spatial_x(coeffs, cosines, sines):
    real_part = coeffs[0].astype(jnp.float32)
    imag_part = coeffs[1].astype(jnp.float32)

    def product(operand, matrix):
        return jnp.einsum("cmk,nk->ncm", operand, matrix, precision=lax.Precision.HIGHEST)

    out_re = product(real_part, cosines) + product(imag_part, sines)
    out_im = product(imag_part, cosines) - product(real_part, sines)
    return jnp.stack([out_re, out_im], axis=1)


def spatial_y(block, cosines, sines, kept):
    shaped = block.reshape(block.shape[0], 2, block.shape[2], kept, block.shape[3] // kept)

    def product(operand, matrix):
        return jnp.einsum("xckp,nk->xpcn", operand, matrix, precision=lax.Precision.HIGHEST)

    out_re = product(shaped[:, 0], cosines) + product(shaped[:, 1], sines)
    out_im = product(shaped[:, 1], cosines) - product(shaped[:, 0], sines)
    return jnp.stack([out_re, out_im], axis=2)


def local_plain(field, cotangent, spectral_weight, local_weight):
    cosines_y, sines_y = phases(field.shape[4], KY)
    low_cosines = cosines_y.astype(jnp.bfloat16)
    low_sines = sines_y.astype(jnp.bfloat16)
    field_rows = spectral_rows(field, low_cosines, low_sines)
    cot_rows = spectral_rows(cotangent, low_cosines, low_sines)
    field_cols = lax.all_to_all(field_rows, "gx", split_axis=3, concat_axis=0, tiled=True)
    cot_cols = lax.all_to_all(cot_rows, "gx", split_axis=3, concat_axis=0, tiled=True)
    cosines_x, sines_x = phases(field_cols.shape[0], spectral_weight.shape[4])
    field_hat = modes_x(field_cols, cosines_x, sines_x)
    cot_hat = modes_x(cot_cols, cosines_x, sines_x)
    mixed, back, grad_spectral = spectral_mix(field_hat, cot_hat, spectral_weight)
    mixed_cols = spatial_x(mixed, cosines_x, sines_x)
    back_cols = spatial_x(back, cosines_x, sines_x)
    mixed_rows = lax.all_to_all(mixed_cols, "gx", split_axis=0, concat_axis=3, tiled=True)
    back_rows = lax.all_to_all(back_cols, "gx", split_axis=0, concat_axis=3, tiled=True)
    local_term = jnp.einsum(
        "xprcn,cd->xprdn", field, local_weight, preferred_element_type=jnp.float32
    )
    output = (spatial_y(mixed_rows, cosines_y, sines_y, KY) + local_term).astype(jnp.bfloat16)
    local_back = jnp.einsum(
        "xprdn,cd->xprcn", cotangent, local_weight, preferred_element_type=jnp.float32
    )
    grad_field = (spatial_y(back_rows, cosines_y, sines_y, KY) + local_back).astype(jnp.bfloat16)
    partial_grad = jnp.einsum(
        "xprcn,xprdn->cd", field, cotangent, preferred_element_type=jnp.float32
    )
    norm_factor = 1.0 / math.sqrt(NX * NY * PAIRS * 2.0)
    grad_local = lax.psum(partial_grad, "gx") * norm_factor
    return (output, grad_field, grad_spectral, grad_local)


LANES = 256
PER = 8
SLOTS = 3
GA = 8
K2 = 48


class Plane:
    @staticmethod
    def a(me, m, sign, n):
        return me ^ m

    @staticmethod
    def b(me, s, sign, n):
        return lax.rem(me + (GA * s * sign + n), n) if not isinstance(me, int) else (me + GA * s * sign) % n


def np_tables(length, kept):
    rows = np.arange(length)[:, None]
    cols = np.arange(kept)[None, :]
    freqs = np.where(cols < kept // 2, cols, cols - kept)
    angles = ((rows * freqs) % length) * (2.0 * np.pi / length)
    return (
        (np.cos(angles) / np.sqrt(length)).astype(np.float32),
        (-np.sin(angles) / np.sqrt(length)).astype(np.float32),
    )


def complex_rows(cos, sin):
    return np.concatenate(
        [
            np.concatenate([cos.T, -sin.T], axis=1),
            np.concatenate([sin.T, cos.T], axis=1),
        ],
        axis=0,
    )


def high_low(array):
    high = array.astype(jnp.bfloat16)
    low = (array - high.astype(np.float32)).astype(jnp.bfloat16)
    return high, low


def x_tables(route, n, cells):
    cos, sin = np_tables(n * cells, 24)
    forward, backward = [], []
    for me in range(n):
        blocks = []
        for m in range(GA):
            source = route.a(me, m, -1, n)
            at = slice(source * cells, (source + 1) * cells)
            blocks.append(complex_rows(cos[at], sin[at]))
        table = np.concatenate(blocks, axis=1)
        high, low = high_low(table)
        forward.append(np.concatenate([high, low, high], axis=1))
        backward.append(np.concatenate([high.T, low.T], axis=1))
    return np.stack(forward), np.stack(backward)


def nt(a, b):
    return lax.dot_general(a, b, (((1,), (1,)), ((), ())), preferred_element_type=F32)


def tn(a, b):
    return lax.dot_general(a, b, (((0,), (0,)), ((), ())), preferred_element_type=F32)


def nn(a, b):
    return lax.dot_general(a, b, (((1,), (0,)), ((), ())), preferred_element_type=F32)


def nn_full(a, b):
    return lax.dot_general(
        a, b, (((1,), (0,)), ((), ())), precision=lax.Precision.HIGHEST, preferred_element_type=F32
    )


def piece_place(route, me, m, s, slot, n):
    owner = route.b(route.a(me, m, 1, n), s, 1, n)
    q = owner * SLOTS + slot
    return q // 4, lax.rem(q, 4)


def rows_kernel(route, n, cells, gb, me_ref, src_ref, tab_ref, *rest):
    outs, hold = rest[:GA], rest[GA]
    x = pl.program_id(0)
    groups = src_ref.shape[1] // PER
    for g in range(groups):
        total = None
        for r in range(2):
            tile = src_ref[0, g * PER : (g + 1) * PER, r].reshape(LANES, src_ref.shape[4])
            part = nt(tab_ref[r], tile)
            total = part if total is None else total + part
        at = pl.ds(pl.multiple_of(x * K2, 8), K2)
        hold[2 * g, at, :] = total[:, :128]
        hold[2 * g + 1, at, :] = total[:, 128:]

    @pl.when(x == cells - 1)
    def _():
        me = me_ref[0]
        for m in range(GA):
            for s in range(gb):
                for slot in range(SLOTS):
                    k, g = piece_place(route, me, m, s, slot, n)
                    for r in range(2):
                        at = (s * SLOTS + slot) * 2 * cells + r * cells
                        for half in range(2):
                            lanes = slice(half * 128, (half + 1) * 128)
                            outs[m][at : at + cells, lanes] = hold[
                                2 * g + half, pl.ds(k + r * KY, cells, stride=K2), :
                            ]


def rows_call(route, n, cells, gb, me, src, tab):
    shape = src.shape
    rows = gb * SLOTS * 2 * cells
    return pl.pallas_call(
        functools.partial(rows_kernel, route, n, cells, gb),
        grid_spec=pltpu.PrefetchScalarGridSpec(
            num_scalar_prefetch=1,
            grid=(cells,),
            in_specs=[
                pl.BlockSpec((1,) + shape[1:], lambda i, me: (i, 0, 0, 0, 0)),
                pl.BlockSpec(tab.shape, lambda i, me: (0, 0, 0)),
            ],
            out_specs=[pl.BlockSpec((rows, LANES), lambda i, me: (0, 0))] * GA,
            scratch_shapes=[pltpu.VMEM((shape[1] // PER * 2, cells * K2, 128), F32)],
        ),
        out_shape=[jax.ShapeDtypeStruct((rows, LANES), F32)] * GA,
        compiler_params=pltpu.CompilerParams(vmem_limit_bytes=24 * 2**20),
        cost_estimate=pl.CostEstimate(flops=int(2e9), bytes_accessed=12 * 2**20, transcendentals=0),
        name="rows",
    )(me, src, tab)


def partial_kernel(cells, gb, me_ref, tab_ref, *rest):
    ins, outs = rest[:GA], rest[GA:]
    table = tab_ref[0]
    step = 2 * cells
    for s in range(gb):
        for slot in range(SLOTS):
            at = (s * SLOTS + slot) * step
            data = jnp.concatenate([ref[at : at + step, :] for ref in ins], axis=0)
            high = data.astype(BF16)
            low = (data - high.astype(F32)).astype(BF16)
            outs[s][slot * K2 : (slot + 1) * K2, :] = nn(
                table, jnp.concatenate([high, high, low], axis=0)
            )


def partial_call(cells, gb, me, tab, messages):
    rows = gb * SLOTS * 2 * cells
    spec = pl.BlockSpec((rows, LANES), lambda i, me: (0, 0))
    out = pl.BlockSpec((SLOTS * K2, LANES), lambda i, me: (0, 0))
    return pl.pallas_call(
        functools.partial(partial_kernel, cells, gb),
        grid_spec=pltpu.PrefetchScalarGridSpec(
            num_scalar_prefetch=1,
            grid=(1,),
            in_specs=[pl.BlockSpec((1,) + tab.shape[1:], lambda i, me: (me[0], 0, 0))] + [spec] * GA,
            out_specs=[out] * gb,
        ),
        out_shape=[jax.ShapeDtypeStruct((SLOTS * K2, LANES), F32)] * gb,
        compiler_params=pltpu.CompilerParams(vmem_limit_bytes=24 * 2**20),
        cost_estimate=pl.CostEstimate(flops=int(1e9), bytes_accessed=4 * 2**20, transcendentals=0),
        name="partial_modes",
    )(me, tab, *messages)


def load_hat(parts, hat_ref, channels):
    for slot in range(SLOTS):
        at = slice(slot * K2, (slot + 1) * K2)
        total = parts[0][at, :]
        for part in parts[1:]:
            total = total + part[at, :]
        total = total.astype(BF16).astype(F32)
        for p in range(PER):
            hat_ref[slot * PER + p] = total[:, p * channels : (p + 1) * channels]


def store_modes(hold, out_ref, channels):
    for slot in range(SLOTS):
        out_ref[slot * K2 : (slot + 1) * K2, :] = jnp.concatenate(
            [hold[slot * PER + p] for p in range(PER)], axis=1
        )


def mix_kernel(gb, block, channels, kx, w_ref, extra_ref, *rest):
    parts, (out_ref, hat_ref, hold) = rest[:gb], rest[gb:]
    i = pl.program_id(0)

    @pl.when(i == 0)
    def _():
        load_hat(parts, hat_ref, channels)

    def body(j, carry):
        mode = i * block + j
        hat_re = hat_ref[mode, 0:kx, :]
        hat_im = hat_ref[mode, kx : 2 * kx, :]
        acc_re = jnp.zeros((kx, channels), F32)
        acc_im = jnp.zeros((kx, channels), F32)
        for c in range(channels):
            w_re = w_ref[0, c, j].astype(F32)
            w_im = w_ref[1, c, j].astype(F32)
            f_re = hat_re[:, c : c + 1]
            f_im = hat_im[:, c : c + 1]
            acc_re += f_re * w_re - f_im * w_im
            acc_im += f_re * w_im + f_im * w_re
        hold[mode, 0:kx, :] = acc_re.astype(BF16).astype(F32)
        hold[mode, kx : 2 * kx, :] = acc_im.astype(BF16).astype(F32)
        return carry

    lax.fori_loop(0, block, body, 0)

    @pl.when(i == pl.num_programs(0) - 1)
    def _():
        store_modes(hold, out_ref, channels)
        out_ref[SLOTS * K2 :, :] = extra_ref[...]


def adjoint_kernel(gb, block, channels, kx, w_ref, *rest):
    parts, (out_ref, hat_ref, hold) = rest[:gb], rest[gb:]
    i = pl.program_id(0)

    @pl.when(i == 0)
    def _():
        load_hat(parts, hat_ref, channels)

    lane = lax.broadcasted_iota(jnp.int32, (kx, channels), 1)

    def body(j, carry):
        mode = i * block + j
        hat_re = hat_ref[mode, 0:kx, :]
        hat_im = hat_ref[mode, kx : 2 * kx, :]
        acc_re = jnp.zeros((kx, channels), F32)
        acc_im = jnp.zeros((kx, channels), F32)
        for c in range(channels):
            w_re = w_ref[0, c, j].astype(F32)
            w_im = w_ref[1, c, j].astype(F32)
            sum_re = jnp.sum(w_re * hat_re + w_im * hat_im, axis=1, keepdims=True)
            sum_im = jnp.sum(w_re * hat_im - w_im * hat_re, axis=1, keepdims=True)
            acc_re = jnp.where(lane == c, sum_re, acc_re)
            acc_im = jnp.where(lane == c, sum_im, acc_im)
        hold[mode, 0:kx, :] = acc_re.astype(BF16).astype(F32)
        hold[mode, kx : 2 * kx, :] = acc_im.astype(BF16).astype(F32)
        return carry

    lax.fori_loop(0, block, body, 0)

    @pl.when(i == pl.num_programs(0) - 1)
    def _():
        store_modes(hold, out_ref, channels)


def mode_call(kernel, name, gb, weight, extra, parts):
    _, channels, modes, kx, _ = weight.shape
    block = 4
    whole = lambda a: pl.BlockSpec(a.shape, lambda i: (0,) * a.ndim)
    more = [extra] if extra is not None else []
    rows = SLOTS * K2 + (extra.shape[0] if extra is not None else 0)
    return pl.pallas_call(
        functools.partial(kernel, gb, block, channels, kx),
        grid=(modes // block,),
        in_specs=[pl.BlockSpec((2, channels, block, kx, channels), lambda i: (0, 0, i, 0, 0))]
        + [whole(a) for a in more]
        + [whole(a) for a in parts],
        out_specs=[
            pl.BlockSpec((rows, LANES), lambda i: (0, 0)),
            pl.BlockSpec((modes, 2 * kx, channels), lambda i: (0, 0, 0)),
        ],
        out_shape=[
            jax.ShapeDtypeStruct((rows, LANES), F32),
            jax.ShapeDtypeStruct((modes, 2 * kx, channels), F32),
        ],
        scratch_shapes=[pltpu.VMEM((modes, 2 * kx, channels), F32)],
        compiler_params=pltpu.CompilerParams(vmem_limit_bytes=32 * 2**20),
        cost_estimate=pl.CostEstimate(flops=int(5e9), bytes_accessed=12 * 2**20, transcendentals=0),
        name=name,
    )(weight, *more, *parts)


def outer_kernel(block, channels, kx, f_ref, g_ref, out_ref):
    def body(j, carry):
        f_re = f_ref[j, 0:kx, :]
        f_im = f_ref[j, kx : 2 * kx, :]
        g_re = g_ref[j, 0:kx, :]
        g_im = g_ref[j, kx : 2 * kx, :]
        for c in range(channels):
            a = f_re[:, c : c + 1]
            b = f_im[:, c : c + 1]
            out_ref[0, c, j] = a * g_re + b * g_im
            out_ref[1, c, j] = a * g_im - b * g_re
        return carry

    lax.fori_loop(0, block, body, 0)


def outer_call(f_hat, g_hat):
    modes, two_kx, channels = f_hat.shape
    kx = two_kx // 2
    block = 4
    spec = pl.BlockSpec((block, two_kx, channels), lambda i: (i, 0, 0))
    return pl.pallas_call(
        functools.partial(outer_kernel, block, channels, kx),
        grid=(modes // block,),
        in_specs=[spec, spec],
        out_specs=pl.BlockSpec((2, channels, block, kx, channels), lambda i: (0, 0, i, 0, 0)),
        out_shape=jax.ShapeDtypeStruct((2, channels, modes, kx, channels), F32),
        compiler_params=pltpu.CompilerParams(vmem_limit_bytes=32 * 2**20),
        cost_estimate=pl.CostEstimate(flops=int(5e9), bytes_accessed=20 * 2**20, transcendentals=0),
        name="grad_modes",
    )(f_hat, g_hat)


def expand_kernel(cells, gb, extra, me_ref, tab_ref, *rest):
    ins, outs = rest[:gb], rest[gb:]
    table = tab_ref[0]
    step = 2 * cells
    for s in range(gb):
        for slot in range(SLOTS):
            data = ins[s][slot * K2 : (slot + 1) * K2, :].astype(BF16)
            full = nn(table, jnp.concatenate([data, data], axis=0))
            at = (s * SLOTS + slot) * step
            for m in range(GA):
                outs[m][at : at + step, :] = full[m * step : (m + 1) * step]
    if extra:
        total = ins[0][SLOTS * K2 :, :]
        for s in range(1, gb):
            total = total + ins[s][SLOTS * K2 :, :]
        for m in range(GA):
            outs[m][gb * SLOTS * step :, :] = total


def expand_call(cells, gb, me, tab, parts):
    extra = parts[0].shape[0] - SLOTS * K2
    rows = gb * SLOTS * 2 * cells + extra
    spec = pl.BlockSpec(parts[0].shape, lambda i, me: (0, 0))
    out = pl.BlockSpec((rows, LANES), lambda i, me: (0, 0))
    return pl.pallas_call(
        functools.partial(expand_kernel, cells, gb, extra),
        grid_spec=pltpu.PrefetchScalarGridSpec(
            num_scalar_prefetch=1,
            grid=(1,),
            in_specs=[pl.BlockSpec((1,) + tab.shape[1:], lambda i, me: (me[0], 0, 0))] + [spec] * gb,
            out_specs=[out] * GA,
        ),
        out_shape=[jax.ShapeDtypeStruct((rows, LANES), F32)] * GA,
        compiler_params=pltpu.CompilerParams(vmem_limit_bytes=24 * 2**20),
        cost_estimate=pl.CostEstimate(flops=int(1e9), bytes_accessed=4 * 2**20, transcendentals=0),
        name="expand_cells",
    )(me, tab, *parts)


def cells_kernel(route, n, cells, gb, extra, me_ref, src_ref, tab_ref, w_ref, *rest):
    ins = rest[:GA]
    out_ref = rest[GA]
    hold = rest[-1]
    x = pl.program_id(0)

    @pl.when(x == 0)
    def _():
        me = me_ref[0]
        for m in range(GA):
            for s in range(gb):
                for slot in range(SLOTS):
                    k, g = piece_place(route, me, m, s, slot, n)
                    for r in range(2):
                        at = (s * SLOTS + slot) * 2 * cells + r * cells
                        for half in range(2):
                            lanes = slice(half * 128, (half + 1) * 128)
                            hold[2 * g + half, pl.ds(k + r * KY, cells, stride=K2), :] = ins[m][
                                at : at + cells, lanes
                            ]
        if extra:
            total = ins[0][gb * SLOTS * 2 * cells :, :]
            for m in range(1, GA):
                total = total + ins[m][gb * SLOTS * 2 * cells :, :]
            rest[GA + 1][...] = total

    for g in range(src_ref.shape[1] // PER):
        at = pl.ds(pl.multiple_of(x * K2, 8), K2)
        data = jnp.concatenate([hold[2 * g, at, :], hold[2 * g + 1, at, :]], axis=1)
        high = data.astype(BF16)
        low = (data - high.astype(F32)).astype(BF16)
        stack = jnp.concatenate([high, high, low], axis=0)
        for r in range(2):
            tile = src_ref[0, g * PER : (g + 1) * PER, r].reshape(LANES, src_ref.shape[4])
            total = tn(stack, tab_ref[r]) + nn(w_ref[...], tile)
            out_ref[0, g * PER : (g + 1) * PER, r] = total.astype(BF16).reshape(
                PER, LANES // PER, src_ref.shape[4]
            )


def cells_call(route, n, cells, gb, me, src, tab, mixer, messages):
    shape = src.shape
    extra = messages[0].shape[0] - gb * SLOTS * 2 * cells
    big = pl.BlockSpec((1,) + shape[1:], lambda i, me: (i, 0, 0, 0, 0))
    whole = lambda a: pl.BlockSpec(a.shape, lambda i, me: (0,) * a.ndim)
    out_specs, out_shape = [big], [jax.ShapeDtypeStruct(shape, BF16)]
    if extra:
        out_specs.append(pl.BlockSpec((extra, LANES), lambda i, me: (0, 0)))
        out_shape.append(jax.ShapeDtypeStruct((extra, LANES), F32))
    return pl.pallas_call(
        functools.partial(cells_kernel, route, n, cells, gb, extra),
        grid_spec=pltpu.PrefetchScalarGridSpec(
            num_scalar_prefetch=1,
            grid=(cells,),
            in_specs=[big, whole(tab), whole(mixer)] + [whole(a) for a in messages],
            out_specs=out_specs,
            scratch_shapes=[pltpu.VMEM((shape[1] // PER * 2, cells * K2, 128), F32)],
        ),
        out_shape=out_shape,
        compiler_params=pltpu.CompilerParams(vmem_limit_bytes=32 * 2**20),
        cost_estimate=pl.CostEstimate(flops=int(4e9), bytes_accessed=20 * 2**20, transcendentals=0),
        name="cells",
    )(me, src, tab, mixer, *messages)


def pointwise_kernel(cells, channels, norm, f_ref, g_ref, out_ref, hold):
    x = pl.program_id(0)
    total = jnp.zeros((LANES, LANES), F32)
    for g in range(f_ref.shape[1] // PER):
        for r in range(2):
            at = slice(g * PER, (g + 1) * PER)
            left = f_ref[0, at, r].reshape(LANES, f_ref.shape[4])
            right = g_ref[0, at, r].reshape(LANES, f_ref.shape[4])
            total = total + nt(left, right)

    @pl.when(x == 0)
    def _():
        hold[...] = total

    @pl.when(x > 0)
    def _():
        hold[...] += total

    @pl.when(x == cells - 1)
    def _():
        iota = lambda shape, dim: lax.broadcasted_iota(jnp.int32, shape, dim)
        square = (LANES, LANES)
        same = iota(square, 0) // channels == iota(square, 1) // channels
        diagonal = jnp.where(same, hold[...], 0.0)
        fold = (iota((channels, LANES), 1) % channels == iota((channels, LANES), 0)).astype(F32)
        rows = nn_full(fold, diagonal)
        spread = (iota(square, 0) % channels == iota(square, 1) % channels).astype(F32)
        full = nn_full(rows, spread)
        keep = iota((channels, LANES), 0) % PER == iota((channels, LANES), 1) // channels
        full = jnp.where(keep, full, 0.0)
        pick = (iota((8, channels), 1) // PER == iota((8, channels), 0)).astype(F32)
        out_ref[...] = nn_full(pick, full) * norm


def pointwise_call(cells, field, cotangent, norm):
    shape = field.shape
    big = pl.BlockSpec((1,) + shape[1:], lambda i: (i, 0, 0, 0, 0))
    return pl.pallas_call(
        functools.partial(pointwise_kernel, cells, shape[3], norm),
        grid=(cells,),
        in_specs=[big, big],
        out_specs=pl.BlockSpec((8, LANES), lambda i: (0, 0)),
        out_shape=jax.ShapeDtypeStruct((8, LANES), F32),
        scratch_shapes=[pltpu.VMEM((LANES, LANES), F32)],
        compiler_params=pltpu.CompilerParams(vmem_limit_bytes=24 * 2**20),
        cost_estimate=pl.CostEstimate(flops=int(4e9), bytes_accessed=17 * 2**20, transcendentals=0),
        name="pointwise",
    )(field, cotangent)


def local_kernels(n, field, cotangent, spectral_weight, local_weight):
    cells = field.shape[0]
    channels = field.shape[3]
    gb = n // GA
    me = lax.axis_index("gx").astype(jnp.int32)[None]
    route_f = Plane
    route_g = Plane

    def send(route, kind, step, sign, array):
        hop = route.a if kind == "a" else route.b
        return lax.ppermute(array, "gx", [(i, hop(i, step, sign, n)) for i in range(n)])

    cos_y, sin_y = np_tables(field.shape[4], KY)
    table_y = complex_rows(cos_y, sin_y)
    split_y = np.stack(np.split(table_y, 2, axis=1))
    rows_table = jnp.asarray(split_y.astype(BF16))
    high, low = high_low(split_y)
    cells_table = jnp.asarray(
        np.concatenate(
            [np.swapaxes(high, 1, 2), np.swapaxes(low, 1, 2), np.swapaxes(high, 1, 2)], axis=2
        ).swapaxes(1, 2)
    )
    forward_f, backward_f = x_tables(route_f, n, cells)
    forward_g, backward_g = (forward_f, backward_f) if route_g is route_f else x_tables(route_g, n, cells)
    eye = jnp.eye(PER, dtype=BF16)
    mixer_g = jnp.kron(eye, local_weight)
    mixer_f = jnp.kron(eye, local_weight.T)
    weight = jnp.transpose(spectral_weight, (0, 1, 3, 4, 2))

    def exchange(route, messages):
        return [messages[0]] + [send(route, "a", m, 1, messages[m]) for m in range(1, GA)]

    def gather(route, parts):
        return [parts[0]] + [send(route, "b", s, 1, parts[s]) for s in range(1, gb)]

    field_rows = exchange(route_f, rows_call(route_f, n, cells, gb, me, field, rows_table))
    cot_rows = exchange(route_g, rows_call(route_g, n, cells, gb, me, cotangent, rows_table))
    norm = 1.0 / math.sqrt(NX * NY * PAIRS * 2.0)
    grad_part = pointwise_call(cells, field, cotangent, norm)

    field_parts = gather(route_f, partial_call(cells, gb, me, jnp.asarray(forward_f), field_rows))
    mixed, field_hat = mode_call(mix_kernel, "mix", gb, weight, grad_part, field_parts)
    cot_parts = gather(route_g, partial_call(cells, gb, me, jnp.asarray(forward_g), cot_rows))
    back, cot_hat = mode_call(adjoint_kernel, "adjoint", gb, weight, None, cot_parts)

    mixed_all = [mixed] + [send(route_f, "b", s, -1, mixed) for s in range(1, gb)]
    back_all = [back] + [send(route_g, "b", s, -1, back) for s in range(1, gb)]
    grad_spectral = jnp.transpose(outer_call(field_hat, cot_hat), (0, 1, 4, 2, 3))

    def exchange_back(route, messages):
        return [messages[0]] + [send(route, "a", m, -1, messages[m]) for m in range(1, GA)]

    mixed_rows = exchange_back(route_f, expand_call(cells, gb, me, jnp.asarray(backward_f), mixed_all))
    back_rows = exchange_back(route_g, expand_call(cells, gb, me, jnp.asarray(backward_g), back_all))
    output, grad_rows = cells_call(
        route_f, n, cells, gb, me, field, cells_table, mixer_f, mixed_rows
    )
    (grad_field,) = cells_call(
        route_g, n, cells, gb, me, cotangent, cells_table, mixer_g, back_rows
    )
    grad_local = grad_rows[: channels // PER].reshape(channels, channels)
    return (output, grad_field, grad_spectral, grad_local)


def solution(mesh):
    n = mesh.shape["gx"]

    def local(field, cotangent, spectral_weight, local_weight):
        tiled = (
            n == 32
            and field.shape == (8, PAIRS, 2, 32, NY)
            and spectral_weight.shape == (2, 32, 32, SLOTS * PER, 24)
        )
        if tiled:
            return local_kernels(n, field, cotangent, spectral_weight, local_weight)
        return local_plain(field, cotangent, spectral_weight, local_weight)

    return jax.shard_map(
        local,
        mesh=mesh,
        in_specs=(
            P(("grp", "gx"), None, None, None, None),
            P(("grp", "gx"), None, None, None, None),
            P(None, None, None, "gx", None),
            P(),
        ),
        out_specs=(
            P(("grp", "gx"), None, None, None, None),
            P(("grp", "gx"), None, None, None, None),
            P(None, None, None, ("grp", "gx"), None),
            P("grp", None),
        ),
        check_vma=False,
    )
```

```python
import functools
import math

import numpy as np

import jax
import jax.numpy as jnp
from jax import lax
from jax.experimental import pallas as pl
from jax.experimental.pallas import tpu as pltpu
from jax.sharding import PartitionSpec as P

NX = 256
NY = 256
KY = 24
PAIRS = 32

F32 = jnp.float32
BF16 = jnp.bfloat16


def phases(length, kept):
    rows_idx = jnp.arange(length, dtype=jnp.int32)[:, None]
    cols_idx = jnp.arange(kept, dtype=jnp.int32)[None, :]
    freqs = jnp.where(cols_idx < kept // 2, cols_idx, cols_idx - kept)
    angles = (rows_idx * freqs % length).astype(jnp.float32) * (2.0 * math.pi / length)
    factor = 1.0 / math.sqrt(length)
    return (jnp.cos(angles) * factor, -jnp.sin(angles) * factor)


def spectral_rows(source, cosines, sines):
    real_part = source[:, :, 0]
    imag_part = source[:, :, 1]

    def product(operand, matrix):
        return jnp.einsum("xpcn,nk->xckp", operand, matrix, preferred_element_type=jnp.float32)

    out_re = product(real_part, cosines) - product(imag_part, sines)
    out_im = product(real_part, sines) + product(imag_part, cosines)
    stacked = jnp.stack([out_re, out_im], axis=1)
    return stacked.reshape(
        stacked.shape[0], 2, stacked.shape[2], stacked.shape[3] * stacked.shape[4]
    )


def modes_x(block, cosines, sines):

    def product(operand, matrix):
        return jnp.einsum("ncm,nk->cmk", operand, matrix, precision=lax.Precision.HIGHEST)

    out_re = product(block[:, 0], cosines) - product(block[:, 1], sines)
    out_im = product(block[:, 0], sines) + product(block[:, 1], cosines)
    return jnp.stack([out_re, out_im]).astype(jnp.bfloat16)


def spectral_mix(coeffs, grads, weights):

    def product(form, left_op, right_op):
        return jnp.einsum(form, left_op, right_op, preferred_element_type=jnp.float32)

    forward_form = "cmk,cdmk->dmk"
    adjoint_form = "dmk,cdmk->cmk"
    outer_form = "cmk,dmk->cdmk"
    mixed_re = product(forward_form, coeffs[0], weights[0]) - product(
        forward_form, coeffs[1], weights[1]
    )
    mixed_im = product(forward_form, coeffs[0], weights[1]) + product(
        forward_form, coeffs[1], weights[0]
    )
    back_re = product(adjoint_form, grads[0], weights[0]) + product(
        adjoint_form, grads[1], weights[1]
    )
    back_im = product(adjoint_form, grads[1], weights[0]) - product(
        adjoint_form, grads[0], weights[1]
    )
    grad_re = product(outer_form, coeffs[0], grads[0]) + product(outer_form, coeffs[1], grads[1])
    grad_im = product(outer_form, coeffs[0], grads[1]) - product(outer_form, coeffs[1], grads[0])
    mixed = jnp.stack([mixed_re, mixed_im]).astype(jnp.bfloat16)
    back = jnp.stack([back_re, back_im]).astype(jnp.bfloat16)
    return (mixed, back, jnp.stack([grad_re, grad_im]))


def spatial_x(coeffs, cosines, sines):
    real_part = coeffs[0].astype(jnp.float32)
    imag_part = coeffs[1].astype(jnp.float32)

    def product(operand, matrix):
        return jnp.einsum("cmk,nk->ncm", operand, matrix, precision=lax.Precision.HIGHEST)

    out_re = product(real_part, cosines) + product(imag_part, sines)
    out_im = product(imag_part, cosines) - product(real_part, sines)
    return jnp.stack([out_re, out_im], axis=1)


def spatial_y(block, cosines, sines, kept):
    shaped = block.reshape(block.shape[0], 2, block.shape[2], kept, block.shape[3] // kept)

    def product(operand, matrix):
        return jnp.einsum("xckp,nk->xpcn", operand, matrix, precision=lax.Precision.HIGHEST)

    out_re = product(shaped[:, 0], cosines) + product(shaped[:, 1], sines)
    out_im = product(shaped[:, 1], cosines) - product(shaped[:, 0], sines)
    return jnp.stack([out_re, out_im], axis=2)


def local_plain(field, cotangent, spectral_weight, local_weight):
    cosines_y, sines_y = phases(field.shape[4], KY)
    low_cosines = cosines_y.astype(jnp.bfloat16)
    low_sines = sines_y.astype(jnp.bfloat16)
    field_rows = spectral_rows(field, low_cosines, low_sines)
    cot_rows = spectral_rows(cotangent, low_cosines, low_sines)
    field_cols = lax.all_to_all(field_rows, "gx", split_axis=3, concat_axis=0, tiled=True)
    cot_cols = lax.all_to_all(cot_rows, "gx", split_axis=3, concat_axis=0, tiled=True)
    cosines_x, sines_x = phases(field_cols.shape[0], spectral_weight.shape[4])
    field_hat = modes_x(field_cols, cosines_x, sines_x)
    cot_hat = modes_x(cot_cols, cosines_x, sines_x)
    mixed, back, grad_spectral = spectral_mix(field_hat, cot_hat, spectral_weight)
    mixed_cols = spatial_x(mixed, cosines_x, sines_x)
    back_cols = spatial_x(back, cosines_x, sines_x)
    mixed_rows = lax.all_to_all(mixed_cols, "gx", split_axis=0, concat_axis=3, tiled=True)
    back_rows = lax.all_to_all(back_cols, "gx", split_axis=0, concat_axis=3, tiled=True)
    local_term = jnp.einsum(
        "xprcn,cd->xprdn", field, local_weight, preferred_element_type=jnp.float32
    )
    output = (spatial_y(mixed_rows, cosines_y, sines_y, KY) + local_term).astype(jnp.bfloat16)
    local_back = jnp.einsum(
        "xprdn,cd->xprcn", cotangent, local_weight, preferred_element_type=jnp.float32
    )
    grad_field = (spatial_y(back_rows, cosines_y, sines_y, KY) + local_back).astype(jnp.bfloat16)
    partial_grad = jnp.einsum(
        "xprcn,xprdn->cd", field, cotangent, preferred_element_type=jnp.float32
    )
    norm_factor = 1.0 / math.sqrt(NX * NY * PAIRS * 2.0)
    grad_local = lax.psum(partial_grad, "gx") * norm_factor
    return (output, grad_field, grad_spectral, grad_local)


LANES = 256
PER = 8
SLOTS = 3
NEAR = 8
G = 4
K2 = 48
CHUNK = SLOTS * K2
EXTRA = 8
MIB = 2**20
VMEM = pl.BlockSpec(memory_space=pltpu.VMEM)
SMEM = pl.BlockSpec(memory_space=pltpu.SMEM)
HBM = pl.BlockSpec(memory_space=pltpu.HBM)


def far(me, s):
    return me ^ (NEAR * s)


def np_tables(length, kept):
    rows = np.arange(length)[:, None]
    cols = np.arange(kept)[None, :]
    freqs = np.where(cols < kept // 2, cols, cols - kept)
    angles = ((rows * freqs) % length) * (2.0 * np.pi / length)
    return (
        (np.cos(angles) / np.sqrt(length)).astype(np.float32),
        (-np.sin(angles) / np.sqrt(length)).astype(np.float32),
    )


def complex_rows(cos, sin):
    return np.concatenate(
        [
            np.concatenate([cos.T, -sin.T], axis=1),
            np.concatenate([sin.T, cos.T], axis=1),
        ],
        axis=0,
    )


def high_low(array):
    high = array.astype(jnp.bfloat16)
    low = (array - high.astype(np.float32)).astype(jnp.bfloat16)
    return high, low


def x_tables(n, cells):
    cos, sin = np_tables(n * cells, 24)
    forward, backward = [], []
    for me in range(n):
        blocks = []
        for m in range(NEAR):
            source = me // NEAR * NEAR + m
            at = slice(source * cells, (source + 1) * cells)
            blocks.append(complex_rows(cos[at], sin[at]))
        table = np.concatenate(blocks, axis=1)
        high, low = high_low(table)
        forward.append(np.concatenate([high, low, high], axis=1))
        backward.append(np.concatenate([high.T, low.T], axis=1))
    return jnp.asarray(np.stack(forward)), jnp.asarray(np.stack(backward))


def nt(a, b):
    return lax.dot_general(a, b, (((1,), (1,)), ((), ())), preferred_element_type=F32)


def tn(a, b):
    return lax.dot_general(a, b, (((0,), (0,)), ((), ())), preferred_element_type=F32)


def nn(a, b):
    return lax.dot_general(a, b, (((1,), (0,)), ((), ())), preferred_element_type=F32)


def nn_full(a, b):
    return lax.dot_general(
        a, b, (((1,), (0,)), ((), ())), precision=lax.Precision.HIGHEST, preferred_element_type=F32
    )


def iota(shape, dim):
    return lax.broadcasted_iota(jnp.int32, shape, dim)


def whole(a):
    return pl.BlockSpec(a.shape, lambda *i: (0,) * a.ndim)


def params(mib):
    return pltpu.CompilerParams(vmem_limit_bytes=mib * MIB)


def cost(flops, mib):
    return pl.CostEstimate(flops=int(flops), bytes_accessed=int(mib * 2**20), transcendentals=0)


def piece_places(me, cells, n):
    for m in range(NEAR):
        for s in range(G):
            owner = far((me & -NEAR) + m, s)
            for slot in range(SLOTS):
                q = owner * SLOTS + slot
                yield m, (s * SLOTS + slot) * 2 * cells, q >> 2, q & 3


def message_shape(cells, extra=0):
    return jax.ShapeDtypeStruct((NEAR * (G * SLOTS * 2 * cells + extra), LANES), F32)


def messages(ref):
    rows = ref.shape[0] // NEAR
    return [ref.at[pl.ds(m * rows, rows)] for m in range(NEAR)]


def fetch(src_ref, buffer, sems):
    def copy(x):
        return pltpu.make_async_copy(src_ref.at[x], buffer.at[x], sems.at[x])

    for x in range(src_ref.shape[0]):
        copy(x).start()
    return copy


def rows_kernel(n, me_ref, src_ref, tab_ref, *rest):
    out_ref, hold, buffer, sems = rest
    outs = messages(out_ref)
    cells, pairs, _, _, length = src_ref.shape
    copy = fetch(src_ref, buffer, sems)

    def body(x, carry):
        copy(x).wait()
        at = pl.ds(pl.multiple_of(x * K2, 8), K2)
        for g in range(pairs // PER):
            total = None
            for r in range(2):
                tile = buffer[x, g * PER : (g + 1) * PER, r].reshape(LANES, length)
                part = nt(tab_ref[r], tile)
                total = part if total is None else total + part
            hold[2 * g, at, :] = total[:, :128]
            hold[2 * g + 1, at, :] = total[:, 128:]
        return carry

    lax.fori_loop(0, cells, body, 0)
    for index, row, k, g in piece_places(me_ref[0], cells, n):
        for r in range(2):
            at = row + r * cells
            for half in range(2):
                outs[index][at : at + cells, half * 128 : (half + 1) * 128] = hold[
                    2 * g + half, pl.ds(k + r * KY, cells, stride=K2), :
                ]


def rows_call(n, me, src, tab):
    cells, pairs = src.shape[:2]
    return pl.pallas_call(
        functools.partial(rows_kernel, n),
        in_specs=[SMEM, HBM, VMEM],
        out_specs=VMEM,
        out_shape=message_shape(cells),
        scratch_shapes=[
            pltpu.VMEM((pairs // PER * 2, cells * K2, 128), F32),
            pltpu.VMEM(src.shape, BF16),
            pltpu.SemaphoreType.DMA((cells,)),
        ],
        compiler_params=params(56),
        cost_estimate=cost(6e9, 14),
        name="rows",
    )(me, src, tab)


def partial_kernel(cells, tab_ref, in_ref, *outs):
    ins = messages(in_ref)
    table = tab_ref[...]
    step = 2 * cells
    for s in range(G):
        for slot in range(SLOTS):
            at = (s * SLOTS + slot) * step
            data = jnp.concatenate([ref[at : at + step, :] for ref in ins], axis=0)
            high = data.astype(BF16)
            low = (data - high.astype(F32)).astype(BF16)
            outs[s][slot * K2 : (slot + 1) * K2, :] = nn(
                table, jnp.concatenate([high, high, low], axis=0)
            )


def partial_call(cells, tab, rows):
    out = [jax.ShapeDtypeStruct((CHUNK, LANES), F32)] * G
    return pl.pallas_call(
        functools.partial(partial_kernel, cells),
        in_specs=[VMEM] * 2,
        out_specs=[VMEM] * G,
        out_shape=out,
        compiler_params=params(16),
        cost_estimate=cost(1e9, 2),
        name="partial_modes",
    )(tab, rows)


def pack_kernel(block, w_ref, out_ref, buffer, sems):
    _, channels, modes, _, _ = w_ref.shape

    def copy(i):
        at = pl.ds(i * block, block)
        return pltpu.make_async_copy(w_ref.at[:, :, at], buffer.at[:, :, at], sems.at[i])

    for i in range(modes // block):
        copy(i).start()

    def body(i, carry):
        copy(i).wait()
        for j in range(block):
            for r in range(2):
                out_ref[r, i * block + j] = jnp.concatenate(
                    [buffer[r, c, i * block + j].astype(F32) for c in range(channels)], axis=1
                )
        return carry

    lax.fori_loop(0, modes // block, body, 0)


def pack_call(weight):
    _, channels, modes, kx, _ = weight.shape
    block = 2
    return pl.pallas_call(
        functools.partial(pack_kernel, block),
        in_specs=[HBM],
        out_specs=VMEM,
        out_shape=jax.ShapeDtypeStruct((2, modes, kx, channels * channels), F32),
        scratch_shapes=[
            pltpu.VMEM(weight.shape, BF16),
            pltpu.SemaphoreType.DMA((modes // block,)),
        ],
        compiler_params=params(55),
        cost_estimate=cost(6e9, 16),
        name="pack_weight",
    )(weight)


def load_hat(parts, hat_ref, channels):
    for slot in range(SLOTS):
        at = slice(slot * K2, (slot + 1) * K2)
        total = parts[0][at, :]
        for part in parts[1:]:
            total = total + part[at, :]
        total = total.astype(BF16).astype(F32)
        for p in range(PER):
            hat_ref[slot * PER + p] = total[:, p * channels : (p + 1) * channels]


def store_modes(hold, out_ref):
    for slot in range(SLOTS):
        out_ref[slot * K2 : (slot + 1) * K2, :] = jnp.concatenate(
            [hold[slot * PER + p] for p in range(PER)], axis=1
        )


BLOCK = 4


def mode_blocks(w_ref, hat_ref, spread_ref, write):
    _, modes, kx, _ = w_ref.shape
    channels = hat_ref.shape[2]

    def body(i, carry):
        at = pl.ds(i * BLOCK, BLOCK)
        hats = hat_ref[at].reshape(BLOCK * 2 * kx, channels).astype(BF16)
        wide = nn(hats, spread_ref[...])
        pieces = []
        for j in range(BLOCK):
            re = wide[2 * j * kx : (2 * j + 1) * kx]
            im = wide[(2 * j + 1) * kx : (2 * j + 2) * kx]
            pieces.append((w_ref[0, i * BLOCK + j], w_ref[1, i * BLOCK + j], re, im))
        write(i, pieces)
        return carry

    lax.fori_loop(0, modes // BLOCK, body, 0)


def mix_kernel(w_ref, spread_ref, extra_ref, *rest):
    parts, (out_ref, hat_ref, hold) = rest[:G], rest[G:]
    channels = hat_ref.shape[2]
    kx = w_ref.shape[2]
    load_hat(parts, hat_ref, channels)

    def fold(value):
        total = value[:, :128]
        for t in range(1, value.shape[1] // 128):
            total = total + value[:, t * 128 : (t + 1) * 128]
        out = total[:, :channels]
        for t in range(1, 128 // channels):
            out = out + total[:, t * channels : (t + 1) * channels]
        return out.astype(BF16).astype(F32)

    def write(i, pieces):
        for j, (w_re, w_im, f_re, f_im) in enumerate(pieces):
            hold[i * BLOCK + j, 0:kx, :] = fold(f_re * w_re - f_im * w_im)
            hold[i * BLOCK + j, kx : 2 * kx, :] = fold(f_re * w_im + f_im * w_re)

    mode_blocks(w_ref, hat_ref, spread_ref, write)
    store_modes(hold, out_ref)
    out_ref[CHUNK:, :] = extra_ref[...]


def adjoint_kernel(w_ref, spread_ref, gather_ref, *rest):
    parts, (out_ref, hat_ref, hold) = rest[:G], rest[G:]
    channels = hat_ref.shape[2]
    kx = w_ref.shape[2]
    load_hat(parts, hat_ref, channels)

    def write(i, pieces):
        both = []
        for w_re, w_im, g_re, g_im in pieces:
            both += [w_re * g_re + w_im * g_im, w_re * g_im - w_im * g_re]
        both = jnp.concatenate(both, axis=0)
        high = both.astype(BF16)
        low = (both - high.astype(F32)).astype(BF16)
        total = nn(high, gather_ref[...]) + nn(low, gather_ref[...])
        hold[pl.ds(i * BLOCK, BLOCK)] = (
            total.astype(BF16).astype(F32).reshape(BLOCK, 2 * kx, channels)
        )

    mode_blocks(w_ref, hat_ref, spread_ref, write)
    store_modes(hold, out_ref)


def mode_call(kernel, name, channels, packed, more, extra, parts):
    _, modes, kx, width = packed.shape
    shape = (modes, 2 * kx, channels)
    return pl.pallas_call(
        kernel,
        in_specs=[VMEM] * (1 + len(more) + len(parts)),
        out_specs=[VMEM] * 2,
        out_shape=[
            jax.ShapeDtypeStruct((CHUNK + extra, LANES), F32),
            jax.ShapeDtypeStruct(shape, F32),
        ],
        scratch_shapes=[pltpu.VMEM(shape, F32)],
        compiler_params=params(16),
        cost_estimate=cost(4e9, 6),
        name=name,
    )(packed, *more, *parts)


def outer_kernel(f_ref, g_ref, out_ref, buffer, sems):
    modes, two_kx, channels = f_ref.shape
    kx = two_kx // 2

    def copy(j):
        return pltpu.make_async_copy(buffer.at[:, :, j], out_ref.at[:, :, j], sems.at[j])

    def body(j, carry):
        f_re = f_ref[j, 0:kx, :]
        f_im = f_ref[j, kx : 2 * kx, :]
        g_re = g_ref[j, 0:kx, :]
        g_im = g_ref[j, kx : 2 * kx, :]
        for c in range(channels):
            a = f_re[:, c : c + 1]
            b = f_im[:, c : c + 1]
            buffer[0, c, j] = a * g_re + b * g_im
            buffer[1, c, j] = a * g_im - b * g_re
        copy(j).start()
        return carry

    def finish(j, carry):
        copy(j).wait()
        return carry

    lax.fori_loop(0, modes, body, 0)
    lax.fori_loop(0, modes, finish, 0)


def outer_call(f_hat, g_hat):
    modes, two_kx, channels = f_hat.shape
    kx = two_kx // 2
    shape = (2, channels, modes, kx, channels)
    return pl.pallas_call(
        outer_kernel,
        in_specs=[VMEM] * 2,
        out_specs=HBM,
        out_shape=jax.ShapeDtypeStruct(shape, F32),
        scratch_shapes=[pltpu.VMEM(shape, F32), pltpu.SemaphoreType.DMA((modes,))],
        compiler_params=params(28),
        cost_estimate=cost(11e9, 34),
        name="grad_modes",
    )(f_hat, g_hat)


def expand_kernel(cells, extra, tab_ref, *rest):
    ins, outs = rest[:G], messages(rest[G])
    table = tab_ref[...]
    step = 2 * cells
    for s in range(G):
        for slot in range(SLOTS):
            data = ins[s][slot * K2 : (slot + 1) * K2, :].astype(BF16)
            full = nn(table, jnp.concatenate([data, data], axis=0))
            at = (s * SLOTS + slot) * step
            for m in range(NEAR):
                outs[m][at : at + step, :] = full[m * step : (m + 1) * step]
    if extra:
        total = ins[0][CHUNK:, :]
        for ref in ins[1:]:
            total = total + ref[CHUNK:, :]
        for m in range(NEAR):
            outs[m][G * SLOTS * step :, :] = total


def expand_call(cells, tab, parts):
    extra = parts[0].shape[0] - CHUNK
    return pl.pallas_call(
        functools.partial(expand_kernel, cells, extra),
        in_specs=[VMEM] * (1 + len(parts)),
        out_specs=VMEM,
        out_shape=message_shape(cells, extra),
        compiler_params=params(16),
        cost_estimate=cost(1e9, 2),
        name="expand_cells",
    )(tab, *parts)


def cells_kernel(n, extra, flip, me_ref, src_ref, tab_ref, w_ref, *rest):
    ins = messages(rest[0])
    out_ref = rest[1]
    hold, mixer, buffer, tiles, in_sems, out_sems = rest[-6:]
    cells, pairs, _, channels, length = src_ref.shape
    copy = fetch(src_ref, buffer, in_sems)

    for index, row, k, g in piece_places(me_ref[0], cells, n):
        for r in range(2):
            at = row + r * cells
            for half in range(2):
                hold[2 * g + half, pl.ds(k + r * KY, cells, stride=K2), :] = ins[index][
                    at : at + cells, half * 128 : (half + 1) * 128
                ]
    if extra:
        at = slice(ins[0].shape[0] - extra, ins[0].shape[0])
        total = ins[0][at, :]
        for ref in ins[1:]:
            total = total + ref[at, :]
        rest[2][...] = total
    tall = (iota((LANES, channels), 0) % channels == iota((LANES, channels), 1)).astype(BF16)
    rows = (nt if flip else nn)(tall, w_ref[...]).astype(BF16)
    same = iota((LANES, LANES), 0) // channels == iota((LANES, LANES), 1) // channels
    mixer[...] = jnp.where(same, nt(rows, tall), 0.0).astype(BF16)

    def copy_out(x):
        return pltpu.make_async_copy(tiles.at[x], out_ref.at[x], out_sems.at[x])

    def body(x, carry):
        copy(x).wait()
        at = pl.ds(pl.multiple_of(x * K2, 8), K2)
        for g in range(pairs // PER):
            data = jnp.concatenate([hold[2 * g, at, :], hold[2 * g + 1, at, :]], axis=1)
            high = data.astype(BF16)
            low = (data - high.astype(F32)).astype(BF16)
            stack = jnp.concatenate([high, high, low], axis=0)
            for r in range(2):
                tile = buffer[x, g * PER : (g + 1) * PER, r].reshape(LANES, length)
                total = tn(stack, tab_ref[r]) + nn(mixer[...], tile)
                tiles[x, g * PER : (g + 1) * PER, r] = total.astype(BF16).reshape(
                    PER, channels, length
                )
        copy_out(x).start()
        return carry

    lax.fori_loop(0, cells, body, 0)
    for x in range(cells):
        copy_out(x).wait()


def cells_call(n, extra, flip, me, src, tab, weight, rows):
    cells, pairs = src.shape[:2]
    out_shape = [jax.ShapeDtypeStruct(src.shape, BF16)]
    if extra:
        out_shape.append(jax.ShapeDtypeStruct((extra, LANES), F32))
    return pl.pallas_call(
        functools.partial(cells_kernel, n, extra, flip),
        in_specs=[SMEM, HBM, VMEM, VMEM, VMEM],
        out_specs=[HBM] + [VMEM] * (len(out_shape) - 1),
        out_shape=out_shape,
        scratch_shapes=[
            pltpu.VMEM((pairs // PER * 2, cells * K2, 128), F32),
            pltpu.VMEM((LANES, LANES), BF16),
            pltpu.VMEM(src.shape, BF16),
            pltpu.VMEM(src.shape, BF16),
            pltpu.SemaphoreType.DMA((cells,)),
            pltpu.SemaphoreType.DMA((cells,)),
        ],
        compiler_params=params(56),
        cost_estimate=cost(9e9, 28),
        name="cells",
    )(me, src, tab, weight, rows)


def pointwise_kernel(norm, f_ref, g_ref, out_ref, f_buffer, g_buffer, hold, f_sems, g_sems):
    cells, pairs, _, channels, length = f_ref.shape
    f_copy = fetch(f_ref, f_buffer, f_sems)
    g_copy = fetch(g_ref, g_buffer, g_sems)
    square = (LANES, LANES)
    hold[...] = jnp.zeros(square, F32)

    def body(x, carry):
        f_copy(x).wait()
        g_copy(x).wait()
        total = hold[...]
        for g in range(pairs // PER):
            at = slice(g * PER, (g + 1) * PER)
            for r in range(2):
                left = f_buffer[x, at, r].reshape(LANES, length)
                right = g_buffer[x, at, r].reshape(LANES, length)
                total = total + nt(left, right)
        hold[...] = total
        return carry

    lax.fori_loop(0, cells, body, 0)
    same = iota(square, 0) // channels == iota(square, 1) // channels
    diagonal = jnp.where(same, hold[...], 0.0)
    fold = (iota((channels, LANES), 1) % channels == iota((channels, LANES), 0)).astype(F32)
    rows = nn_full(fold, diagonal)
    spread = (iota(square, 0) % channels == iota(square, 1) % channels).astype(F32)
    full = nn_full(rows, spread)
    keep = iota((channels, LANES), 0) % PER == iota((channels, LANES), 1) // channels
    full = jnp.where(keep, full, 0.0)
    pick = (iota((EXTRA, channels), 1) // PER == iota((EXTRA, channels), 0)).astype(F32)
    out_ref[...] = nn_full(pick, full) * norm


def pointwise_call(field, cotangent, norm):
    cells = field.shape[0]
    return pl.pallas_call(
        functools.partial(pointwise_kernel, norm),
        in_specs=[HBM] * 2,
        out_specs=VMEM,
        out_shape=jax.ShapeDtypeStruct((EXTRA, LANES), F32),
        scratch_shapes=[
            pltpu.VMEM(field.shape, BF16),
            pltpu.VMEM(field.shape, BF16),
            pltpu.VMEM((LANES, LANES), F32),
            pltpu.SemaphoreType.DMA((cells,)),
            pltpu.SemaphoreType.DMA((cells,)),
        ],
        compiler_params=params(56),
        cost_estimate=cost(8e9, 20),
        name="pointwise",
    )(field, cotangent)


def local_kernels(n, field, cotangent, spectral_weight, local_weight):
    cells = field.shape[0]
    channels = field.shape[3]
    me = lax.axis_index("gx").astype(jnp.int32)[None]

    def permute(array, hop):
        return lax.ppermute(array, "gx", [(i, hop(i)) for i in range(n)])

    planes = [list(range(first, first + NEAR)) for first in range(0, n, NEAR)]

    def near_exchange(rows):
        stacked = rows.reshape(NEAR, rows.shape[0] // NEAR, LANES)
        moved = lax.all_to_all(stacked, "gx", 0, 0, axis_index_groups=planes, tiled=True)
        return moved.reshape(rows.shape)

    def hop(array, s):
        return permute(array, lambda i: far(i, s))

    def far_scatter(parts):
        return [parts[0]] + [hop(parts[s], s) for s in (1, 2, 3)]

    def far_gather(chunk):
        got = hop(chunk, 2)
        return [chunk, hop(chunk, 1), got, hop(got, 1)]

    cos_y, sin_y = np_tables(field.shape[4], KY)
    split_y = np.stack(np.split(complex_rows(cos_y, sin_y), 2, axis=1))
    rows_table = jnp.asarray(split_y.astype(BF16))
    high, low = high_low(split_y)
    cells_table = jnp.asarray(np.concatenate([high, low, high], axis=1))
    def own(table):
        return lax.dynamic_index_in_dim(table, me[0], 0, keepdims=False)

    forward, backward = map(own, x_tables(n, cells))
    lanes = np.arange(channels * channels)
    index = np.arange(channels)[:, None]
    by_c = jnp.asarray((lanes // channels == index).astype(np.float32).astype(BF16))
    by_d = jnp.asarray((lanes % channels == index).astype(np.float32).astype(BF16))
    gather_c = jnp.asarray((lanes // channels == index).astype(np.float32).T.astype(BF16))
    weight = jnp.transpose(spectral_weight, (0, 1, 3, 4, 2))
    norm = 1.0 / math.sqrt(NX * NY * PAIRS * 2.0)

    def after(arrays, *others):
        return lax.optimization_barrier((arrays, others))[0]

    field_rows = near_exchange(rows_call(n, me, field, rows_table))
    cot_out = rows_call(n, me, cotangent, rows_table)
    grad_part = pointwise_call(after(field, cot_out), cotangent, norm)
    packed = pack_call(after(weight, grad_part))

    field_sums = partial_call(cells, forward, after(field_rows, packed))
    field_parts = far_scatter(field_sums)
    cot_rows = near_exchange(after(cot_out, field_sums))
    mixed, field_hat = mode_call(
        mix_kernel, "mix", channels, packed, [by_c, grad_part], EXTRA, field_parts
    )
    cot_sums = partial_call(cells, forward, after(cot_rows, mixed))
    cot_parts = far_scatter(cot_sums)
    mixed_parts = after(far_gather(mixed), cot_parts)
    mixed_rows = near_exchange(expand_call(cells, backward, mixed_parts))
    back, cot_hat = mode_call(
        adjoint_kernel, "adjoint", channels, packed, [by_d, gather_c], 0, cot_parts
    )
    outer = outer_call(field_hat, after(cot_hat, back))
    grad_spectral = jnp.transpose(outer, (0, 1, 4, 2, 3))
    back_parts = far_gather(back)
    back_rows = near_exchange(expand_call(cells, backward, back_parts))
    output, grad_rows = cells_call(
        n, EXTRA, True, me, field, cells_table, local_weight, mixed_rows
    )
    (grad_field,) = cells_call(
        n, 0, False, me, cotangent, cells_table, local_weight, back_rows
    )
    grad_local = grad_rows[: channels // PER].reshape(channels, channels)
    return (output, grad_field, grad_spectral, grad_local)


def solution(mesh):
    n = mesh.shape["gx"]

    def local(field, cotangent, spectral_weight, local_weight):
        tiled = (
            n == 32
            and field.shape == (8, PAIRS, 2, 32, NY)
            and spectral_weight.shape == (2, 32, 32, SLOTS * PER, 24)
        )
        if tiled:
            return local_kernels(n, field, cotangent, spectral_weight, local_weight)
        return local_plain(field, cotangent, spectral_weight, local_weight)

    return jax.shard_map(
        local,
        mesh=mesh,
        in_specs=(
            P(("grp", "gx"), None, None, None, None),
            P(("grp", "gx"), None, None, None, None),
            P(None, None, None, "gx", None),
            P(),
        ),
        out_specs=(
            P(("grp", "gx"), None, None, None, None),
            P(("grp", "gx"), None, None, None, None),
            P(None, None, None, ("grp", "gx"), None),
            P("grp", None),
        ),
        check_vma=False,
    )
```

```python
import functools
import math

import numpy as np

import jax
import jax.numpy as jnp
from jax import lax
from jax.experimental import pallas as pl
from jax.experimental.pallas import tpu as pltpu
from jax.sharding import PartitionSpec as P

NX = 256
NY = 256
KY = 24
PAIRS = 32

F32 = jnp.float32
BF16 = jnp.bfloat16


def phases(length, kept):
    rows_idx = jnp.arange(length, dtype=jnp.int32)[:, None]
    cols_idx = jnp.arange(kept, dtype=jnp.int32)[None, :]
    freqs = jnp.where(cols_idx < kept // 2, cols_idx, cols_idx - kept)
    angles = (rows_idx * freqs % length).astype(jnp.float32) * (2.0 * math.pi / length)
    factor = 1.0 / math.sqrt(length)
    return (jnp.cos(angles) * factor, -jnp.sin(angles) * factor)


def spectral_rows(source, cosines, sines):
    real_part = source[:, :, 0]
    imag_part = source[:, :, 1]

    def product(operand, matrix):
        return jnp.einsum("xpcn,nk->xckp", operand, matrix, preferred_element_type=jnp.float32)

    out_re = product(real_part, cosines) - product(imag_part, sines)
    out_im = product(real_part, sines) + product(imag_part, cosines)
    stacked = jnp.stack([out_re, out_im], axis=1)
    return stacked.reshape(
        stacked.shape[0], 2, stacked.shape[2], stacked.shape[3] * stacked.shape[4]
    )


def modes_x(block, cosines, sines):

    def product(operand, matrix):
        return jnp.einsum("ncm,nk->cmk", operand, matrix, precision=lax.Precision.HIGHEST)

    out_re = product(block[:, 0], cosines) - product(block[:, 1], sines)
    out_im = product(block[:, 0], sines) + product(block[:, 1], cosines)
    return jnp.stack([out_re, out_im]).astype(jnp.bfloat16)


def spectral_mix(coeffs, grads, weights):

    def product(form, left_op, right_op):
        return jnp.einsum(form, left_op, right_op, preferred_element_type=jnp.float32)

    forward_form = "cmk,cdmk->dmk"
    adjoint_form = "dmk,cdmk->cmk"
    outer_form = "cmk,dmk->cdmk"
    mixed_re = product(forward_form, coeffs[0], weights[0]) - product(
        forward_form, coeffs[1], weights[1]
    )
    mixed_im = product(forward_form, coeffs[0], weights[1]) + product(
        forward_form, coeffs[1], weights[0]
    )
    back_re = product(adjoint_form, grads[0], weights[0]) + product(
        adjoint_form, grads[1], weights[1]
    )
    back_im = product(adjoint_form, grads[1], weights[0]) - product(
        adjoint_form, grads[0], weights[1]
    )
    grad_re = product(outer_form, coeffs[0], grads[0]) + product(outer_form, coeffs[1], grads[1])
    grad_im = product(outer_form, coeffs[0], grads[1]) - product(outer_form, coeffs[1], grads[0])
    mixed = jnp.stack([mixed_re, mixed_im]).astype(jnp.bfloat16)
    back = jnp.stack([back_re, back_im]).astype(jnp.bfloat16)
    return (mixed, back, jnp.stack([grad_re, grad_im]))


def spatial_x(coeffs, cosines, sines):
    real_part = coeffs[0].astype(jnp.float32)
    imag_part = coeffs[1].astype(jnp.float32)

    def product(operand, matrix):
        return jnp.einsum("cmk,nk->ncm", operand, matrix, precision=lax.Precision.HIGHEST)

    out_re = product(real_part, cosines) + product(imag_part, sines)
    out_im = product(imag_part, cosines) - product(real_part, sines)
    return jnp.stack([out_re, out_im], axis=1)


def spatial_y(block, cosines, sines, kept):
    shaped = block.reshape(block.shape[0], 2, block.shape[2], kept, block.shape[3] // kept)

    def product(operand, matrix):
        return jnp.einsum("xckp,nk->xpcn", operand, matrix, precision=lax.Precision.HIGHEST)

    out_re = product(shaped[:, 0], cosines) + product(shaped[:, 1], sines)
    out_im = product(shaped[:, 1], cosines) - product(shaped[:, 0], sines)
    return jnp.stack([out_re, out_im], axis=2)


def local_plain(field, cotangent, spectral_weight, local_weight):
    cosines_y, sines_y = phases(field.shape[4], KY)
    low_cosines = cosines_y.astype(jnp.bfloat16)
    low_sines = sines_y.astype(jnp.bfloat16)
    field_rows = spectral_rows(field, low_cosines, low_sines)
    cot_rows = spectral_rows(cotangent, low_cosines, low_sines)
    field_cols = lax.all_to_all(field_rows, "gx", split_axis=3, concat_axis=0, tiled=True)
    cot_cols = lax.all_to_all(cot_rows, "gx", split_axis=3, concat_axis=0, tiled=True)
    cosines_x, sines_x = phases(field_cols.shape[0], spectral_weight.shape[4])
    field_hat = modes_x(field_cols, cosines_x, sines_x)
    cot_hat = modes_x(cot_cols, cosines_x, sines_x)
    mixed, back, grad_spectral = spectral_mix(field_hat, cot_hat, spectral_weight)
    mixed_cols = spatial_x(mixed, cosines_x, sines_x)
    back_cols = spatial_x(back, cosines_x, sines_x)
    mixed_rows = lax.all_to_all(mixed_cols, "gx", split_axis=0, concat_axis=3, tiled=True)
    back_rows = lax.all_to_all(back_cols, "gx", split_axis=0, concat_axis=3, tiled=True)
    local_term = jnp.einsum(
        "xprcn,cd->xprdn", field, local_weight, preferred_element_type=jnp.float32
    )
    output = (spatial_y(mixed_rows, cosines_y, sines_y, KY) + local_term).astype(jnp.bfloat16)
    local_back = jnp.einsum(
        "xprdn,cd->xprcn", cotangent, local_weight, preferred_element_type=jnp.float32
    )
    grad_field = (spatial_y(back_rows, cosines_y, sines_y, KY) + local_back).astype(jnp.bfloat16)
    partial_grad = jnp.einsum(
        "xprcn,xprdn->cd", field, cotangent, preferred_element_type=jnp.float32
    )
    norm_factor = 1.0 / math.sqrt(NX * NY * PAIRS * 2.0)
    grad_local = lax.psum(partial_grad, "gx") * norm_factor
    return (output, grad_field, grad_spectral, grad_local)


LANES = 256
PER = 8
SLOTS = 3
NEAR = 8
G = 4
K2 = 48
CHUNK = SLOTS * K2
EXTRA = 8
MIB = 2**20
VMEM = pl.BlockSpec(memory_space=pltpu.VMEM)
SMEM = pl.BlockSpec(memory_space=pltpu.SMEM)
HBM = pl.BlockSpec(memory_space=pltpu.HBM)


def far(me, s):
    return me ^ (NEAR * s)


def np_tables(length, kept):
    rows = np.arange(length)[:, None]
    cols = np.arange(kept)[None, :]
    freqs = np.where(cols < kept // 2, cols, cols - kept)
    angles = ((rows * freqs) % length) * (2.0 * np.pi / length)
    return (
        (np.cos(angles) / np.sqrt(length)).astype(np.float32),
        (-np.sin(angles) / np.sqrt(length)).astype(np.float32),
    )


def complex_rows(cos, sin):
    return np.concatenate(
        [
            np.concatenate([cos.T, -sin.T], axis=1),
            np.concatenate([sin.T, cos.T], axis=1),
        ],
        axis=0,
    )


def high_low(array):
    high = array.astype(jnp.bfloat16)
    low = (array - high.astype(np.float32)).astype(jnp.bfloat16)
    return high, low


def x_tables(n, cells):
    cos, sin = np_tables(n * cells, 24)
    forward, backward = [], []
    for me in range(n):
        blocks = []
        for m in range(NEAR):
            source = me // NEAR * NEAR + m
            at = slice(source * cells, (source + 1) * cells)
            blocks.append(complex_rows(cos[at], sin[at]))
        table = np.concatenate(blocks, axis=1)
        high, low = high_low(table)
        forward.append(np.concatenate([high, low, high], axis=1))
        backward.append(np.concatenate([high.T, low.T], axis=1))
    return jnp.asarray(np.stack(forward)), jnp.asarray(np.stack(backward))


def nt(a, b):
    return lax.dot_general(a, b, (((1,), (1,)), ((), ())), preferred_element_type=F32)


def tn(a, b):
    return lax.dot_general(a, b, (((0,), (0,)), ((), ())), preferred_element_type=F32)


def nn(a, b):
    return lax.dot_general(a, b, (((1,), (0,)), ((), ())), preferred_element_type=F32)


def nn_full(a, b):
    return lax.dot_general(
        a, b, (((1,), (0,)), ((), ())), precision=lax.Precision.HIGHEST, preferred_element_type=F32
    )


def iota(shape, dim):
    return lax.broadcasted_iota(jnp.int32, shape, dim)


def whole(a):
    return pl.BlockSpec(a.shape, lambda *i: (0,) * a.ndim)


def params(mib):
    return pltpu.CompilerParams(vmem_limit_bytes=mib * MIB)


def cost(flops, mib):
    return pl.CostEstimate(flops=int(flops), bytes_accessed=int(mib * 2**20), transcendentals=0)


def piece_places(me, cells, n):
    for m in range(NEAR):
        for s in range(G):
            owner = far((me & -NEAR) + m, s)
            for slot in range(SLOTS):
                q = owner * SLOTS + slot
                yield m, (s * SLOTS + slot) * 2 * cells, q >> 2, q & 3


def message_shape(cells, extra=0):
    return jax.ShapeDtypeStruct((NEAR * (G * SLOTS * 2 * cells + extra), LANES), F32)


def messages(ref):
    rows = ref.shape[0] // NEAR
    return [ref.at[pl.ds(m * rows, rows)] for m in range(NEAR)]


def fetch(src_ref, buffer, sems):
    def copy(x):
        return pltpu.make_async_copy(src_ref.at[x], buffer.at[x], sems.at[x])

    for x in range(src_ref.shape[0]):
        copy(x).start()
    return copy


def rows_kernel(n, me_ref, src_ref, tab_ref, *rest):
    out_ref, hold, buffer, sems = rest
    outs = messages(out_ref)
    cells, pairs, _, _, length = src_ref.shape
    copy = fetch(src_ref, buffer, sems)

    def body(x, carry):
        copy(x).wait()
        at = pl.ds(pl.multiple_of(x * K2, 8), K2)
        for g in range(pairs // PER):
            total = None
            for r in range(2):
                tile = buffer[x, g * PER : (g + 1) * PER, r].reshape(LANES, length)
                part = nt(tab_ref[r], tile)
                total = part if total is None else total + part
            hold[2 * g, at, :] = total[:, :128]
            hold[2 * g + 1, at, :] = total[:, 128:]
        return carry

    lax.fori_loop(0, cells, body, 0)
    for index, row, k, g in piece_places(me_ref[0], cells, n):
        for r in range(2):
            at = row + r * cells
            for half in range(2):
                outs[index][at : at + cells, half * 128 : (half + 1) * 128] = hold[
                    2 * g + half, pl.ds(k + r * KY, cells, stride=K2), :
                ]


def rows_call(n, me, src, tab):
    cells, pairs = src.shape[:2]
    return pl.pallas_call(
        functools.partial(rows_kernel, n),
        in_specs=[SMEM, HBM, VMEM],
        out_specs=VMEM,
        out_shape=message_shape(cells),
        scratch_shapes=[
            pltpu.VMEM((pairs // PER * 2, cells * K2, 128), F32),
            pltpu.VMEM(src.shape, BF16),
            pltpu.SemaphoreType.DMA((cells,)),
        ],
        compiler_params=params(56),
        cost_estimate=cost(6e9, 14),
        name="rows",
    )(me, src, tab)


def partial_kernel(cells, tab_ref, in_ref, *outs):
    ins = messages(in_ref)
    table = tab_ref[...]
    step = 2 * cells
    for s in range(G):
        for slot in range(SLOTS):
            at = (s * SLOTS + slot) * step
            data = jnp.concatenate([ref[at : at + step, :] for ref in ins], axis=0)
            high = data.astype(BF16)
            low = (data - high.astype(F32)).astype(BF16)
            outs[s][slot * K2 : (slot + 1) * K2, :] = nn(
                table, jnp.concatenate([high, high, low], axis=0)
            )


def partial_call(cells, tab, rows):
    out = [jax.ShapeDtypeStruct((CHUNK, LANES), F32)] * G
    return pl.pallas_call(
        functools.partial(partial_kernel, cells),
        in_specs=[VMEM] * 2,
        out_specs=[VMEM] * G,
        out_shape=out,
        compiler_params=params(16),
        cost_estimate=cost(1e9, 2),
        name="partial_modes",
    )(tab, rows)


def pack_kernel(block, w_ref, out_ref, buffer, sems):
    _, channels, modes, _, _ = w_ref.shape

    def copy(i):
        at = pl.ds(i * block, block)
        return pltpu.make_async_copy(w_ref.at[:, :, at], buffer.at[:, :, at], sems.at[i])

    for i in range(modes // block):
        copy(i).start()

    def body(i, carry):
        copy(i).wait()
        for j in range(block):
            for r in range(2):
                out_ref[r, i * block + j] = jnp.concatenate(
                    [buffer[r, c, i * block + j].astype(F32) for c in range(channels)], axis=1
                ).astype(BF16)
        return carry

    lax.fori_loop(0, modes // block, body, 0)


def pack_call(weight):
    _, channels, modes, kx, _ = weight.shape
    block = 2
    return pl.pallas_call(
        functools.partial(pack_kernel, block),
        in_specs=[HBM],
        out_specs=VMEM,
        out_shape=jax.ShapeDtypeStruct((2, modes, kx, channels * channels), BF16),
        scratch_shapes=[
            pltpu.VMEM(weight.shape, BF16),
            pltpu.SemaphoreType.DMA((modes // block,)),
        ],
        compiler_params=params(55),
        cost_estimate=cost(6e9, 16),
        name="pack_weight",
    )(weight)


def load_hat(parts, hat_ref, channels):
    for slot in range(SLOTS):
        at = slice(slot * K2, (slot + 1) * K2)
        total = parts[0][at, :]
        for part in parts[1:]:
            total = total + part[at, :]
        total = total.astype(BF16).astype(F32)
        for p in range(PER):
            hat_ref[slot * PER + p] = total[:, p * channels : (p + 1) * channels]


def store_modes(hold, out_ref):
    for slot in range(SLOTS):
        out_ref[slot * K2 : (slot + 1) * K2, :] = jnp.concatenate(
            [hold[slot * PER + p] for p in range(PER)], axis=1
        )


BLOCK = 4


def mode_blocks(w_ref, hat_ref, spread_ref, write):
    _, modes, kx, _ = w_ref.shape
    channels = hat_ref.shape[2]

    def body(i, carry):
        at = pl.ds(i * BLOCK, BLOCK)
        hats = hat_ref[at].reshape(BLOCK * 2 * kx, channels).astype(BF16)
        wide = nn(hats, spread_ref[...])
        pieces = []
        for j in range(BLOCK):
            re = wide[2 * j * kx : (2 * j + 1) * kx]
            im = wide[(2 * j + 1) * kx : (2 * j + 2) * kx]
            mode = i * BLOCK + j
            pieces.append((w_ref[0, mode].astype(F32), w_ref[1, mode].astype(F32), re, im))
        write(i, pieces)
        return carry

    lax.fori_loop(0, modes // BLOCK, body, 0)


def mix_kernel(w_ref, spread_ref, extra_ref, *rest):
    parts, (out_ref, hat_ref, hold) = rest[:G], rest[G:]
    channels = hat_ref.shape[2]
    kx = w_ref.shape[2]
    load_hat(parts, hat_ref, channels)

    def fold(value):
        total = value[:, :128]
        for t in range(1, value.shape[1] // 128):
            total = total + value[:, t * 128 : (t + 1) * 128]
        out = total[:, :channels]
        for t in range(1, 128 // channels):
            out = out + total[:, t * channels : (t + 1) * channels]
        return out.astype(BF16).astype(F32)

    def write(i, pieces):
        for j, (w_re, w_im, f_re, f_im) in enumerate(pieces):
            hold[i * BLOCK + j, 0:kx, :] = fold(f_re * w_re - f_im * w_im)
            hold[i * BLOCK + j, kx : 2 * kx, :] = fold(f_re * w_im + f_im * w_re)

    mode_blocks(w_ref, hat_ref, spread_ref, write)
    store_modes(hold, out_ref)
    out_ref[CHUNK:, :] = extra_ref[...]


def adjoint_kernel(w_ref, spread_ref, gather_ref, *rest):
    parts, (out_ref, hat_ref, hold) = rest[:G], rest[G:]
    channels = hat_ref.shape[2]
    kx = w_ref.shape[2]
    load_hat(parts, hat_ref, channels)

    def write(i, pieces):
        both = []
        for w_re, w_im, g_re, g_im in pieces:
            both += [w_re * g_re + w_im * g_im, w_re * g_im - w_im * g_re]
        both = jnp.concatenate(both, axis=0)
        high = both.astype(BF16)
        low = (both - high.astype(F32)).astype(BF16)
        total = nn(high, gather_ref[...]) + nn(low, gather_ref[...])
        hold[pl.ds(i * BLOCK, BLOCK)] = (
            total.astype(BF16).astype(F32).reshape(BLOCK, 2 * kx, channels)
        )

    mode_blocks(w_ref, hat_ref, spread_ref, write)
    store_modes(hold, out_ref)


def mode_call(kernel, name, channels, packed, more, extra, parts):
    _, modes, kx, width = packed.shape
    shape = (modes, 2 * kx, channels)
    return pl.pallas_call(
        kernel,
        in_specs=[VMEM] * (1 + len(more) + len(parts)),
        out_specs=[VMEM] * 2,
        out_shape=[
            jax.ShapeDtypeStruct((CHUNK + extra, LANES), F32),
            jax.ShapeDtypeStruct(shape, F32),
        ],
        scratch_shapes=[pltpu.VMEM(shape, F32)],
        compiler_params=params(16),
        cost_estimate=cost(4e9, 6),
        name=name,
    )(packed, *more, *parts)


def outer_kernel(f_ref, g_ref, out_ref, buffer, sems):
    modes, two_kx, channels = f_ref.shape
    kx = two_kx // 2

    def copy(j):
        return pltpu.make_async_copy(buffer.at[:, :, j], out_ref.at[:, :, j], sems.at[j])

    def body(j, carry):
        f_re = f_ref[j, 0:kx, :]
        f_im = f_ref[j, kx : 2 * kx, :]
        g_re = g_ref[j, 0:kx, :]
        g_im = g_ref[j, kx : 2 * kx, :]
        for c in range(channels):
            a = f_re[:, c : c + 1]
            b = f_im[:, c : c + 1]
            buffer[0, c, j] = a * g_re + b * g_im
            buffer[1, c, j] = a * g_im - b * g_re
        copy(j).start()
        return carry

    def finish(j, carry):
        copy(j).wait()
        return carry

    lax.fori_loop(0, modes, body, 0)
    lax.fori_loop(0, modes, finish, 0)


def outer_call(f_hat, g_hat):
    modes, two_kx, channels = f_hat.shape
    kx = two_kx // 2
    shape = (2, channels, modes, kx, channels)
    return pl.pallas_call(
        outer_kernel,
        in_specs=[VMEM] * 2,
        out_specs=HBM,
        out_shape=jax.ShapeDtypeStruct(shape, F32),
        scratch_shapes=[pltpu.VMEM(shape, F32), pltpu.SemaphoreType.DMA((modes,))],
        compiler_params=params(28),
        cost_estimate=cost(11e9, 34),
        name="grad_modes",
    )(f_hat, g_hat)


def expand_kernel(cells, extra, tab_ref, *rest):
    ins, outs = rest[:G], messages(rest[G])
    table = tab_ref[...]
    step = 2 * cells
    for s in range(G):
        for slot in range(SLOTS):
            data = ins[s][slot * K2 : (slot + 1) * K2, :].astype(BF16)
            full = nn(table, jnp.concatenate([data, data], axis=0))
            at = (s * SLOTS + slot) * step
            for m in range(NEAR):
                outs[m][at : at + step, :] = full[m * step : (m + 1) * step]
    if extra:
        total = ins[0][CHUNK:, :]
        for ref in ins[1:]:
            total = total + ref[CHUNK:, :]
        for m in range(NEAR):
            outs[m][G * SLOTS * step :, :] = total


def expand_call(cells, tab, parts):
    extra = parts[0].shape[0] - CHUNK
    return pl.pallas_call(
        functools.partial(expand_kernel, cells, extra),
        in_specs=[VMEM] * (1 + len(parts)),
        out_specs=VMEM,
        out_shape=message_shape(cells, extra),
        compiler_params=params(16),
        cost_estimate=cost(1e9, 2),
        name="expand_cells",
    )(tab, *parts)


def cells_kernel(n, extra, flip, me_ref, src_ref, tab_ref, w_ref, *rest):
    ins = messages(rest[0])
    out_ref = rest[1]
    hold, mixer, buffer, tiles, in_sems, out_sems = rest[-6:]
    cells, pairs, _, channels, length = src_ref.shape
    copy = fetch(src_ref, buffer, in_sems)

    for index, row, k, g in piece_places(me_ref[0], cells, n):
        for r in range(2):
            at = row + r * cells
            for half in range(2):
                hold[2 * g + half, pl.ds(k + r * KY, cells, stride=K2), :] = ins[index][
                    at : at + cells, half * 128 : (half + 1) * 128
                ]
    if extra:
        at = slice(ins[0].shape[0] - extra, ins[0].shape[0])
        total = ins[0][at, :]
        for ref in ins[1:]:
            total = total + ref[at, :]
        for c in range(channels):
            lanes = slice(c % PER * channels, (c % PER + 1) * channels)
            rest[2][c : c + 1, :] = total[c // PER : c // PER + 1, lanes]
    tall = (iota((LANES, channels), 0) % channels == iota((LANES, channels), 1)).astype(BF16)
    rows = (nt if flip else nn)(tall, w_ref[...]).astype(BF16)
    same = iota((LANES, LANES), 0) // channels == iota((LANES, LANES), 1) // channels
    mixer[...] = jnp.where(same, nt(rows, tall), 0.0).astype(BF16)

    def copy_out(x):
        return pltpu.make_async_copy(tiles.at[x], out_ref.at[x], out_sems.at[x])

    def body(x, carry):
        copy(x).wait()
        at = pl.ds(pl.multiple_of(x * K2, 8), K2)
        for g in range(pairs // PER):
            data = jnp.concatenate([hold[2 * g, at, :], hold[2 * g + 1, at, :]], axis=1)
            high = data.astype(BF16)
            low = (data - high.astype(F32)).astype(BF16)
            stack = jnp.concatenate([high, high, low], axis=0)
            for r in range(2):
                tile = buffer[x, g * PER : (g + 1) * PER, r].reshape(LANES, length)
                total = tn(stack, tab_ref[r]) + nn(mixer[...], tile)
                tiles[x, g * PER : (g + 1) * PER, r] = total.astype(BF16).reshape(
                    PER, channels, length
                )
        copy_out(x).start()
        return carry

    lax.fori_loop(0, cells, body, 0)
    for x in range(cells):
        copy_out(x).wait()


def cells_call(n, extra, flip, me, src, tab, weight, rows):
    cells, pairs = src.shape[:2]
    out_shape = [jax.ShapeDtypeStruct(src.shape, BF16)]
    if extra:
        out_shape.append(jax.ShapeDtypeStruct(weight.shape, F32))
    return pl.pallas_call(
        functools.partial(cells_kernel, n, extra, flip),
        in_specs=[SMEM, HBM, VMEM, VMEM, VMEM],
        out_specs=[HBM] + [VMEM] * (len(out_shape) - 1),
        out_shape=out_shape,
        scratch_shapes=[
            pltpu.VMEM((pairs // PER * 2, cells * K2, 128), F32),
            pltpu.VMEM((LANES, LANES), BF16),
            pltpu.VMEM(src.shape, BF16),
            pltpu.VMEM(src.shape, BF16),
            pltpu.SemaphoreType.DMA((cells,)),
            pltpu.SemaphoreType.DMA((cells,)),
        ],
        compiler_params=params(56),
        cost_estimate=cost(9e9, 28),
        name="cells",
    )(me, src, tab, weight, rows)


def rows_pointwise_kernel(n, norm, me_ref, field_ref, src_ref, tab_ref, *rest):
    out_ref, grad_ref, hold, square, f_buffer, buffer, f_sems, sems = rest
    outs = messages(out_ref)
    cells, pairs, _, channels, length = src_ref.shape
    copy = fetch(src_ref, buffer, sems)
    f_copy = fetch(field_ref, f_buffer, f_sems)
    square[...] = jnp.zeros(square.shape, F32)

    def body(x, carry):
        copy(x).wait()
        f_copy(x).wait()
        at = pl.ds(pl.multiple_of(x * K2, 8), K2)
        products = square[...]
        for g in range(pairs // PER):
            total = None
            for r in range(2):
                tile = buffer[x, g * PER : (g + 1) * PER, r].reshape(LANES, length)
                left = f_buffer[x, g * PER : (g + 1) * PER, r].reshape(LANES, length)
                products = products + nt(left, tile)
                part = nt(tab_ref[r], tile)
                total = part if total is None else total + part
            hold[2 * g, at, :] = total[:, :128]
            hold[2 * g + 1, at, :] = total[:, 128:]
        square[...] = products
        return carry

    lax.fori_loop(0, cells, body, 0)
    for index, row, k, g in piece_places(me_ref[0], cells, n):
        for r in range(2):
            at = row + r * cells
            for half in range(2):
                outs[index][at : at + cells, half * 128 : (half + 1) * 128] = hold[
                    2 * g + half, pl.ds(k + r * KY, cells, stride=K2), :
                ]
    shape = (LANES, LANES)
    same = iota(shape, 0) // channels == iota(shape, 1) // channels
    diagonal = jnp.where(same, square[...], 0.0)
    fold = (iota((channels, LANES), 1) % channels == iota((channels, LANES), 0)).astype(F32)
    rows = nn_full(fold, diagonal)
    spread = (iota(shape, 0) % channels == iota(shape, 1) % channels).astype(F32)
    full = nn_full(rows, spread)
    keep = iota((channels, LANES), 0) % PER == iota((channels, LANES), 1) // channels
    full = jnp.where(keep, full, 0.0)
    pick = (iota((EXTRA, channels), 1) // PER == iota((EXTRA, channels), 0)).astype(F32)
    grad_ref[...] = nn_full(pick, full) * norm


def rows_pointwise_call(n, norm, me, field, src, tab):
    cells, pairs = src.shape[:2]
    return pl.pallas_call(
        functools.partial(rows_pointwise_kernel, n, norm),
        in_specs=[SMEM, HBM, HBM, VMEM],
        out_specs=[VMEM] * 2,
        out_shape=[message_shape(cells), jax.ShapeDtypeStruct((EXTRA, LANES), F32)],
        scratch_shapes=[
            pltpu.VMEM((pairs // PER * 2, cells * K2, 128), F32),
            pltpu.VMEM((LANES, LANES), F32),
            pltpu.VMEM(src.shape, BF16),
            pltpu.VMEM(src.shape, BF16),
            pltpu.SemaphoreType.DMA((cells,)),
            pltpu.SemaphoreType.DMA((cells,)),
        ],
        compiler_params=params(56),
        cost_estimate=cost(14e9, 34),
        name="rows_pointwise",
    )(me, field, src, tab)


def local_kernels(n, field, cotangent, spectral_weight, local_weight):
    cells = field.shape[0]
    channels = field.shape[3]
    me = lax.axis_index("gx").astype(jnp.int32)[None]

    def permute(array, hop):
        return lax.ppermute(array, "gx", [(i, hop(i)) for i in range(n)])

    planes = [list(range(first, first + NEAR)) for first in range(0, n, NEAR)]

    def near_exchange(rows):
        stacked = rows.reshape(NEAR, rows.shape[0] // NEAR, LANES)
        moved = lax.all_to_all(stacked, "gx", 0, 0, axis_index_groups=planes, tiled=True)
        return moved.reshape(rows.shape)

    def hop(array, s):
        return permute(array, lambda i: far(i, s))

    def far_scatter(parts):
        return [parts[0]] + [hop(parts[s], s) for s in (1, 2, 3)]

    def far_gather(chunk):
        got = hop(chunk, 2)
        return [chunk, hop(chunk, 1), got, hop(got, 1)]

    cos_y, sin_y = np_tables(field.shape[4], KY)
    split_y = np.stack(np.split(complex_rows(cos_y, sin_y), 2, axis=1))
    rows_table = jnp.asarray(split_y.astype(BF16))
    high, low = high_low(split_y)
    cells_table = jnp.asarray(np.concatenate([high, low, high], axis=1))
    def own(table):
        return lax.dynamic_index_in_dim(table, me[0], 0, keepdims=False)

    forward, backward = map(own, x_tables(n, cells))
    lanes = np.arange(channels * channels)
    index = np.arange(channels)[:, None]
    by_c = jnp.asarray((lanes // channels == index).astype(np.float32).astype(BF16))
    by_d = jnp.asarray((lanes % channels == index).astype(np.float32).astype(BF16))
    gather_c = jnp.asarray((lanes // channels == index).astype(np.float32).T.astype(BF16))
    weight = jnp.transpose(spectral_weight, (0, 1, 3, 4, 2))
    norm = 1.0 / math.sqrt(NX * NY * PAIRS * 2.0)

    def after(arrays, *others):
        return lax.optimization_barrier((arrays, others))[0]

    field_out = rows_call(n, me, field, rows_table)
    field_rows = near_exchange(field_out)
    cot_out, grad_part = rows_pointwise_call(
        n, norm, me, after(field, field_out), cotangent, rows_table
    )
    packed = pack_call(after(weight, grad_part))

    field_sums = partial_call(cells, forward, after(field_rows, packed))
    field_parts = far_scatter(field_sums)
    cot_rows = near_exchange(after(cot_out, field_sums))
    mixed, field_hat = mode_call(
        mix_kernel, "mix", channels, packed, [by_c, grad_part], EXTRA, field_parts
    )
    cot_sums = partial_call(cells, forward, after(cot_rows, mixed))
    cot_parts = far_scatter(cot_sums)
    mixed_parts = after(far_gather(mixed), cot_parts)
    mixed_rows = near_exchange(expand_call(cells, backward, mixed_parts))
    back, cot_hat = mode_call(
        adjoint_kernel, "adjoint", channels, packed, [by_d, gather_c], 0, cot_parts
    )
    outer = outer_call(field_hat, after(cot_hat, back))
    grad_spectral = jnp.transpose(outer, (0, 1, 4, 2, 3))
    back_parts = far_gather(back)
    back_rows = near_exchange(expand_call(cells, backward, back_parts))
    output, grad_local = cells_call(
        n, EXTRA, True, me, field, cells_table, local_weight, mixed_rows
    )
    (grad_field,) = cells_call(
        n, 0, False, me, cotangent, cells_table, local_weight, back_rows
    )
    return (output, grad_field, grad_spectral, grad_local)


def solution(mesh):
    n = mesh.shape["gx"]

    def local(field, cotangent, spectral_weight, local_weight):
        tiled = (
            n == 32
            and field.shape == (8, PAIRS, 2, 32, NY)
            and spectral_weight.shape == (2, 32, 32, SLOTS * PER, 24)
        )
        if tiled:
            return local_kernels(n, field, cotangent, spectral_weight, local_weight)
        return local_plain(field, cotangent, spectral_weight, local_weight)

    return jax.shard_map(
        local,
        mesh=mesh,
        in_specs=(
            P(("grp", "gx"), None, None, None, None),
            P(("grp", "gx"), None, None, None, None),
            P(None, None, None, "gx", None),
            P(),
        ),
        out_specs=(
            P(("grp", "gx"), None, None, None, None),
            P(("grp", "gx"), None, None, None, None),
            P(None, None, None, ("grp", "gx"), None),
            P("grp", None),
        ),
        check_vma=False,
    )
```

```python
import functools
import math

import numpy as np

import jax
import jax.numpy as jnp
from jax import lax
from jax.experimental import pallas as pl
from jax.experimental.pallas import tpu as pltpu
from jax.sharding import PartitionSpec as P

NX = 256
NY = 256
KY = 24
PAIRS = 32

F32 = jnp.float32
BF16 = jnp.bfloat16


def phases(length, kept):
    rows_idx = jnp.arange(length, dtype=jnp.int32)[:, None]
    cols_idx = jnp.arange(kept, dtype=jnp.int32)[None, :]
    freqs = jnp.where(cols_idx < kept // 2, cols_idx, cols_idx - kept)
    angles = (rows_idx * freqs % length).astype(jnp.float32) * (2.0 * math.pi / length)
    factor = 1.0 / math.sqrt(length)
    return (jnp.cos(angles) * factor, -jnp.sin(angles) * factor)


def spectral_rows(source, cosines, sines):
    real_part = source[:, :, 0]
    imag_part = source[:, :, 1]

    def product(operand, matrix):
        return jnp.einsum("xpcn,nk->xckp", operand, matrix, preferred_element_type=jnp.float32)

    out_re = product(real_part, cosines) - product(imag_part, sines)
    out_im = product(real_part, sines) + product(imag_part, cosines)
    stacked = jnp.stack([out_re, out_im], axis=1)
    return stacked.reshape(
        stacked.shape[0], 2, stacked.shape[2], stacked.shape[3] * stacked.shape[4]
    )


def modes_x(block, cosines, sines):

    def product(operand, matrix):
        return jnp.einsum("ncm,nk->cmk", operand, matrix, precision=lax.Precision.HIGHEST)

    out_re = product(block[:, 0], cosines) - product(block[:, 1], sines)
    out_im = product(block[:, 0], sines) + product(block[:, 1], cosines)
    return jnp.stack([out_re, out_im]).astype(jnp.bfloat16)


def spectral_mix(coeffs, grads, weights):

    def product(form, left_op, right_op):
        return jnp.einsum(form, left_op, right_op, preferred_element_type=jnp.float32)

    forward_form = "cmk,cdmk->dmk"
    adjoint_form = "dmk,cdmk->cmk"
    outer_form = "cmk,dmk->cdmk"
    mixed_re = product(forward_form, coeffs[0], weights[0]) - product(
        forward_form, coeffs[1], weights[1]
    )
    mixed_im = product(forward_form, coeffs[0], weights[1]) + product(
        forward_form, coeffs[1], weights[0]
    )
    back_re = product(adjoint_form, grads[0], weights[0]) + product(
        adjoint_form, grads[1], weights[1]
    )
    back_im = product(adjoint_form, grads[1], weights[0]) - product(
        adjoint_form, grads[0], weights[1]
    )
    grad_re = product(outer_form, coeffs[0], grads[0]) + product(outer_form, coeffs[1], grads[1])
    grad_im = product(outer_form, coeffs[0], grads[1]) - product(outer_form, coeffs[1], grads[0])
    mixed = jnp.stack([mixed_re, mixed_im]).astype(jnp.bfloat16)
    back = jnp.stack([back_re, back_im]).astype(jnp.bfloat16)
    return (mixed, back, jnp.stack([grad_re, grad_im]))


def spatial_x(coeffs, cosines, sines):
    real_part = coeffs[0].astype(jnp.float32)
    imag_part = coeffs[1].astype(jnp.float32)

    def product(operand, matrix):
        return jnp.einsum("cmk,nk->ncm", operand, matrix, precision=lax.Precision.HIGHEST)

    out_re = product(real_part, cosines) + product(imag_part, sines)
    out_im = product(imag_part, cosines) - product(real_part, sines)
    return jnp.stack([out_re, out_im], axis=1)


def spatial_y(block, cosines, sines, kept):
    shaped = block.reshape(block.shape[0], 2, block.shape[2], kept, block.shape[3] // kept)

    def product(operand, matrix):
        return jnp.einsum("xckp,nk->xpcn", operand, matrix, precision=lax.Precision.HIGHEST)

    out_re = product(shaped[:, 0], cosines) + product(shaped[:, 1], sines)
    out_im = product(shaped[:, 1], cosines) - product(shaped[:, 0], sines)
    return jnp.stack([out_re, out_im], axis=2)


def local_plain(field, cotangent, spectral_weight, local_weight):
    cosines_y, sines_y = phases(field.shape[4], KY)
    low_cosines = cosines_y.astype(jnp.bfloat16)
    low_sines = sines_y.astype(jnp.bfloat16)
    field_rows = spectral_rows(field, low_cosines, low_sines)
    cot_rows = spectral_rows(cotangent, low_cosines, low_sines)
    field_cols = lax.all_to_all(field_rows, "gx", split_axis=3, concat_axis=0, tiled=True)
    cot_cols = lax.all_to_all(cot_rows, "gx", split_axis=3, concat_axis=0, tiled=True)
    cosines_x, sines_x = phases(field_cols.shape[0], spectral_weight.shape[4])
    field_hat = modes_x(field_cols, cosines_x, sines_x)
    cot_hat = modes_x(cot_cols, cosines_x, sines_x)
    mixed, back, grad_spectral = spectral_mix(field_hat, cot_hat, spectral_weight)
    mixed_cols = spatial_x(mixed, cosines_x, sines_x)
    back_cols = spatial_x(back, cosines_x, sines_x)
    mixed_rows = lax.all_to_all(mixed_cols, "gx", split_axis=0, concat_axis=3, tiled=True)
    back_rows = lax.all_to_all(back_cols, "gx", split_axis=0, concat_axis=3, tiled=True)
    local_term = jnp.einsum(
        "xprcn,cd->xprdn", field, local_weight, preferred_element_type=jnp.float32
    )
    output = (spatial_y(mixed_rows, cosines_y, sines_y, KY) + local_term).astype(jnp.bfloat16)
    local_back = jnp.einsum(
        "xprdn,cd->xprcn", cotangent, local_weight, preferred_element_type=jnp.float32
    )
    grad_field = (spatial_y(back_rows, cosines_y, sines_y, KY) + local_back).astype(jnp.bfloat16)
    partial_grad = jnp.einsum(
        "xprcn,xprdn->cd", field, cotangent, preferred_element_type=jnp.float32
    )
    norm_factor = 1.0 / math.sqrt(NX * NY * PAIRS * 2.0)
    grad_local = lax.psum(partial_grad, "gx") * norm_factor
    return (output, grad_field, grad_spectral, grad_local)


LANES = 256
PER = 8
SLOTS = 3
NEAR = 8
G = 4
K2 = 48
CHUNK = SLOTS * K2
EXTRA = 8
MIB = 2**20
VMEM = pl.BlockSpec(memory_space=pltpu.VMEM)
SMEM = pl.BlockSpec(memory_space=pltpu.SMEM)
HBM = pl.BlockSpec(memory_space=pltpu.HBM)


def far(me, s):
    return me ^ (NEAR * s)


def np_tables(length, kept):
    rows = np.arange(length)[:, None]
    cols = np.arange(kept)[None, :]
    freqs = np.where(cols < kept // 2, cols, cols - kept)
    angles = ((rows * freqs) % length) * (2.0 * np.pi / length)
    return (
        (np.cos(angles) / np.sqrt(length)).astype(np.float32),
        (-np.sin(angles) / np.sqrt(length)).astype(np.float32),
    )


def complex_rows(cos, sin):
    return np.concatenate(
        [
            np.concatenate([cos.T, -sin.T], axis=1),
            np.concatenate([sin.T, cos.T], axis=1),
        ],
        axis=0,
    )


def high_low(array):
    high = array.astype(jnp.bfloat16)
    low = (array - high.astype(np.float32)).astype(jnp.bfloat16)
    return high, low


def x_tables(n, cells):
    cos, sin = np_tables(n * cells, 24)
    forward, backward = [], []
    for me in range(n):
        blocks = []
        for m in range(NEAR):
            source = me // NEAR * NEAR + m
            at = slice(source * cells, (source + 1) * cells)
            blocks.append(complex_rows(cos[at], sin[at]))
        table = np.concatenate(blocks, axis=1)
        high, low = high_low(table)
        forward.append(np.concatenate([high, low, high], axis=1))
        backward.append(np.concatenate([high.T, low.T], axis=1))
    return jnp.asarray(np.stack(forward)), jnp.asarray(np.stack(backward))


def nt(a, b):
    return lax.dot_general(a, b, (((1,), (1,)), ((), ())), preferred_element_type=F32)


def tn(a, b):
    return lax.dot_general(a, b, (((0,), (0,)), ((), ())), preferred_element_type=F32)


def nn(a, b):
    return lax.dot_general(a, b, (((1,), (0,)), ((), ())), preferred_element_type=F32)


def nn_full(a, b):
    return lax.dot_general(
        a, b, (((1,), (0,)), ((), ())), precision=lax.Precision.HIGHEST, preferred_element_type=F32
    )


def iota(shape, dim):
    return lax.broadcasted_iota(jnp.int32, shape, dim)


def whole(a):
    return pl.BlockSpec(a.shape, lambda *i: (0,) * a.ndim)


def params(mib):
    return pltpu.CompilerParams(vmem_limit_bytes=mib * MIB)


def cost(flops, mib):
    return pl.CostEstimate(flops=int(flops), bytes_accessed=int(mib * 2**20), transcendentals=0)


def piece_places(me, cells, n):
    for m in range(NEAR):
        for s in range(G):
            owner = far((me & -NEAR) + m, s)
            for slot in range(SLOTS):
                q = owner * SLOTS + slot
                yield m, (s * SLOTS + slot) * 2 * cells, q >> 2, q & 3


def message_shape(cells, extra=0):
    return jax.ShapeDtypeStruct((NEAR * (G * SLOTS * 2 * cells + extra), LANES), F32)


def messages(ref):
    rows = ref.shape[0] // NEAR
    return [ref.at[pl.ds(m * rows, rows)] for m in range(NEAR)]


def fetch(src_ref, buffer, sems):
    def copy(x):
        return pltpu.make_async_copy(src_ref.at[x], buffer.at[x], sems.at[x])

    for x in range(src_ref.shape[0]):
        copy(x).start()
    return copy


def departures(stage, out_ref, sems):
    pairs = zip(messages(stage), messages(out_ref))
    return [pltpu.make_async_copy(a, b, sems.at[m]) for m, (a, b) in enumerate(pairs)]


def rows_kernel(n, me_ref, src_ref, tab_ref, *rest):
    out_ref, hold, buffer, sems, stage, out_sems = rest
    outs = messages(stage)
    leave = departures(stage, out_ref, out_sems)
    cells, pairs, _, _, length = src_ref.shape
    copy = fetch(src_ref, buffer, sems)

    def body(x, carry):
        copy(x).wait()
        at = pl.ds(pl.multiple_of(x * K2, 8), K2)
        for g in range(pairs // PER):
            total = None
            for r in range(2):
                tile = buffer[x, g * PER : (g + 1) * PER, r].reshape(LANES, length)
                part = nt(tab_ref[r], tile)
                total = part if total is None else total + part
            hold[2 * g, at, :] = total[:, :128]
            hold[2 * g + 1, at, :] = total[:, 128:]
        return carry

    lax.fori_loop(0, cells, body, 0)
    for index, row, k, g in piece_places(me_ref[0], cells, n):
        if row == 0 and index > 0:
            leave[index - 1].start()
        for r in range(2):
            at = row + r * cells
            for half in range(2):
                outs[index][at : at + cells, half * 128 : (half + 1) * 128] = hold[
                    2 * g + half, pl.ds(k + r * KY, cells, stride=K2), :
                ]
    leave[-1].start()
    for copy in leave:
        copy.wait()


def rows_call(n, me, src, tab):
    cells, pairs = src.shape[:2]
    return pl.pallas_call(
        functools.partial(rows_kernel, n),
        in_specs=[SMEM, HBM, VMEM],
        out_specs=HBM,
        out_shape=message_shape(cells),
        scratch_shapes=[
            pltpu.VMEM((pairs // PER * 2, cells * K2, 128), F32),
            pltpu.VMEM(src.shape, BF16),
            pltpu.SemaphoreType.DMA((cells,)),
            pltpu.VMEM(message_shape(cells).shape, F32),
            pltpu.SemaphoreType.DMA((NEAR,)),
        ],
        compiler_params=params(56),
        cost_estimate=cost(6e9, 14),
        name="rows",
    )(me, src, tab)


def partial_kernel(cells, tab_ref, in_ref, *outs):
    ins = messages(in_ref)
    table = tab_ref[...]
    step = 2 * cells
    for s in range(G):
        for slot in range(SLOTS):
            at = (s * SLOTS + slot) * step
            data = jnp.concatenate([ref[at : at + step, :] for ref in ins], axis=0)
            high = data.astype(BF16)
            low = (data - high.astype(F32)).astype(BF16)
            outs[s][slot * K2 : (slot + 1) * K2, :] = nn(
                table, jnp.concatenate([high, high, low], axis=0)
            )


def partial_call(cells, tab, rows):
    out = [jax.ShapeDtypeStruct((CHUNK, LANES), F32)] * G
    return pl.pallas_call(
        functools.partial(partial_kernel, cells),
        in_specs=[VMEM] * 2,
        out_specs=[VMEM] * G,
        out_shape=out,
        compiler_params=params(16),
        cost_estimate=cost(1e9, 2),
        name="partial_modes",
    )(tab, rows)


def pack_kernel(block, w_ref, out_ref, buffer, sems):
    _, channels, modes, _, _ = w_ref.shape

    def copy(i):
        at = pl.ds(i * block, block)
        return pltpu.make_async_copy(w_ref.at[:, :, at], buffer.at[:, :, at], sems.at[i])

    for i in range(modes // block):
        copy(i).start()

    def body(i, carry):
        copy(i).wait()
        for j in range(block):
            for r in range(2):
                out_ref[r, i * block + j] = jnp.concatenate(
                    [buffer[r, c, i * block + j].astype(F32) for c in range(channels)], axis=1
                ).astype(BF16)
        return carry

    lax.fori_loop(0, modes // block, body, 0)


def pack_call(weight):
    _, channels, modes, kx, _ = weight.shape
    block = 2
    return pl.pallas_call(
        functools.partial(pack_kernel, block),
        in_specs=[HBM],
        out_specs=VMEM,
        out_shape=jax.ShapeDtypeStruct((2, modes, kx, channels * channels), BF16),
        scratch_shapes=[
            pltpu.VMEM(weight.shape, BF16),
            pltpu.SemaphoreType.DMA((modes // block,)),
        ],
        compiler_params=params(55),
        cost_estimate=cost(6e9, 16),
        name="pack_weight",
    )(weight)


def load_hat(parts, hat_ref, channels):
    for slot in range(SLOTS):
        at = slice(slot * K2, (slot + 1) * K2)
        total = parts[0][at, :]
        for part in parts[1:]:
            total = total + part[at, :]
        total = total.astype(BF16).astype(F32)
        for p in range(PER):
            hat_ref[slot * PER + p] = total[:, p * channels : (p + 1) * channels]


def store_modes(hold, out_ref):
    for slot in range(SLOTS):
        out_ref[slot * K2 : (slot + 1) * K2, :] = jnp.concatenate(
            [hold[slot * PER + p] for p in range(PER)], axis=1
        )


BLOCK = 4


def mode_blocks(w_ref, hat_ref, spread_ref, write):
    _, modes, kx, _ = w_ref.shape
    channels = hat_ref.shape[2]

    def body(i, carry):
        at = pl.ds(i * BLOCK, BLOCK)
        hats = hat_ref[at].reshape(BLOCK * 2 * kx, channels).astype(BF16)
        wide = nn(hats, spread_ref[...])
        pieces = []
        for j in range(BLOCK):
            re = wide[2 * j * kx : (2 * j + 1) * kx]
            im = wide[(2 * j + 1) * kx : (2 * j + 2) * kx]
            mode = i * BLOCK + j
            pieces.append((w_ref[0, mode].astype(F32), w_ref[1, mode].astype(F32), re, im))
        write(i, pieces)
        return carry

    lax.fori_loop(0, modes // BLOCK, body, 0)


def mix_kernel(w_ref, spread_ref, extra_ref, *rest):
    parts, (out_ref, hat_ref, hold) = rest[:G], rest[G:]
    channels = hat_ref.shape[2]
    kx = w_ref.shape[2]
    load_hat(parts, hat_ref, channels)

    def fold(value):
        total = value[:, :128]
        for t in range(1, value.shape[1] // 128):
            total = total + value[:, t * 128 : (t + 1) * 128]
        out = total[:, :channels]
        for t in range(1, 128 // channels):
            out = out + total[:, t * channels : (t + 1) * channels]
        return out.astype(BF16).astype(F32)

    def write(i, pieces):
        for j, (w_re, w_im, f_re, f_im) in enumerate(pieces):
            hold[i * BLOCK + j, 0:kx, :] = fold(f_re * w_re - f_im * w_im)
            hold[i * BLOCK + j, kx : 2 * kx, :] = fold(f_re * w_im + f_im * w_re)

    mode_blocks(w_ref, hat_ref, spread_ref, write)
    store_modes(hold, out_ref)
    out_ref[CHUNK:, :] = extra_ref[...]


def adjoint_kernel(w_ref, spread_ref, gather_ref, *rest):
    parts, (out_ref, hat_ref, hold) = rest[:G], rest[G:]
    channels = hat_ref.shape[2]
    kx = w_ref.shape[2]
    load_hat(parts, hat_ref, channels)

    def write(i, pieces):
        both = []
        for w_re, w_im, g_re, g_im in pieces:
            both += [w_re * g_re + w_im * g_im, w_re * g_im - w_im * g_re]
        both = jnp.concatenate(both, axis=0)
        high = both.astype(BF16)
        low = (both - high.astype(F32)).astype(BF16)
        total = nn(high, gather_ref[...]) + nn(low, gather_ref[...])
        hold[pl.ds(i * BLOCK, BLOCK)] = (
            total.astype(BF16).astype(F32).reshape(BLOCK, 2 * kx, channels)
        )

    mode_blocks(w_ref, hat_ref, spread_ref, write)
    store_modes(hold, out_ref)


def mode_call(kernel, name, channels, packed, more, extra, parts):
    _, modes, kx, width = packed.shape
    shape = (modes, 2 * kx, channels)
    return pl.pallas_call(
        kernel,
        in_specs=[VMEM] * (1 + len(more) + len(parts)),
        out_specs=[VMEM] * 2,
        out_shape=[
            jax.ShapeDtypeStruct((CHUNK + extra, LANES), F32),
            jax.ShapeDtypeStruct(shape, F32),
        ],
        scratch_shapes=[pltpu.VMEM(shape, F32)],
        compiler_params=params(16),
        cost_estimate=cost(4e9, 6),
        name=name,
    )(packed, *more, *parts)


def outer_kernel(f_ref, g_ref, out_ref, buffer, sems):
    modes, two_kx, channels = f_ref.shape
    kx = two_kx // 2

    def copy(j):
        return pltpu.make_async_copy(buffer.at[:, :, j], out_ref.at[:, :, j], sems.at[j])

    def body(j, carry):
        f_re = f_ref[j, 0:kx, :]
        f_im = f_ref[j, kx : 2 * kx, :]
        g_re = g_ref[j, 0:kx, :]
        g_im = g_ref[j, kx : 2 * kx, :]
        for c in range(channels):
            a = f_re[:, c : c + 1]
            b = f_im[:, c : c + 1]
            buffer[0, c, j] = a * g_re + b * g_im
            buffer[1, c, j] = a * g_im - b * g_re
        copy(j).start()
        return carry

    def finish(j, carry):
        copy(j).wait()
        return carry

    lax.fori_loop(0, modes, body, 0)
    lax.fori_loop(0, modes, finish, 0)


def outer_call(f_hat, g_hat):
    modes, two_kx, channels = f_hat.shape
    kx = two_kx // 2
    shape = (2, channels, modes, kx, channels)
    return pl.pallas_call(
        outer_kernel,
        in_specs=[VMEM] * 2,
        out_specs=HBM,
        out_shape=jax.ShapeDtypeStruct(shape, F32),
        scratch_shapes=[pltpu.VMEM(shape, F32), pltpu.SemaphoreType.DMA((modes,))],
        compiler_params=params(28),
        cost_estimate=cost(11e9, 34),
        name="grad_modes",
    )(f_hat, g_hat)


def expand_kernel(cells, extra, tab_ref, *rest):
    ins, (out_ref, stage, out_sems) = rest[:G], rest[G:]
    outs = messages(stage)
    leave = departures(stage, out_ref, out_sems)
    table = tab_ref[...]
    step = 2 * cells
    for s in range(G):
        for slot in range(SLOTS):
            data = ins[s][slot * K2 : (slot + 1) * K2, :].astype(BF16)
            full = nn(table, jnp.concatenate([data, data], axis=0))
            at = (s * SLOTS + slot) * step
            for m in range(NEAR):
                outs[m][at : at + step, :] = full[m * step : (m + 1) * step]
    if extra:
        total = ins[0][CHUNK:, :]
        for ref in ins[1:]:
            total = total + ref[CHUNK:, :]
        for m in range(NEAR):
            outs[m][G * SLOTS * step :, :] = total
    for copy in leave:
        copy.start()
    for copy in leave:
        copy.wait()


def expand_call(cells, tab, parts):
    extra = parts[0].shape[0] - CHUNK
    return pl.pallas_call(
        functools.partial(expand_kernel, cells, extra),
        in_specs=[VMEM] * (1 + len(parts)),
        out_specs=HBM,
        out_shape=message_shape(cells, extra),
        scratch_shapes=[
            pltpu.VMEM(message_shape(cells, extra).shape, F32),
            pltpu.SemaphoreType.DMA((NEAR,)),
        ],
        compiler_params=params(16),
        cost_estimate=cost(1e9, 2),
        name="expand_cells",
    )(tab, *parts)


def cells_kernel(n, extra, flip, me_ref, src_ref, tab_ref, w_ref, *rest):
    ins = messages(rest[0])
    out_ref = rest[1]
    hold, mixer, buffer, tiles, in_sems, out_sems = rest[-6:]
    cells, pairs, _, channels, length = src_ref.shape
    copy = fetch(src_ref, buffer, in_sems)

    for index, row, k, g in piece_places(me_ref[0], cells, n):
        for r in range(2):
            at = row + r * cells
            for half in range(2):
                hold[2 * g + half, pl.ds(k + r * KY, cells, stride=K2), :] = ins[index][
                    at : at + cells, half * 128 : (half + 1) * 128
                ]
    if extra:
        at = slice(ins[0].shape[0] - extra, ins[0].shape[0])
        total = ins[0][at, :]
        for ref in ins[1:]:
            total = total + ref[at, :]
        for c in range(channels):
            lanes = slice(c % PER * channels, (c % PER + 1) * channels)
            rest[2][c : c + 1, :] = total[c // PER : c // PER + 1, lanes]
    tall = (iota((LANES, channels), 0) % channels == iota((LANES, channels), 1)).astype(BF16)
    rows = (nt if flip else nn)(tall, w_ref[...]).astype(BF16)
    same = iota((LANES, LANES), 0) // channels == iota((LANES, LANES), 1) // channels
    mixer[...] = jnp.where(same, nt(rows, tall), 0.0).astype(BF16)

    def copy_out(x):
        return pltpu.make_async_copy(tiles.at[x], out_ref.at[x], out_sems.at[x])

    def body(x, carry):
        copy(x).wait()
        at = pl.ds(pl.multiple_of(x * K2, 8), K2)
        for g in range(pairs // PER):
            data = jnp.concatenate([hold[2 * g, at, :], hold[2 * g + 1, at, :]], axis=1)
            high = data.astype(BF16)
            low = (data - high.astype(F32)).astype(BF16)
            stack = jnp.concatenate([high, high, low], axis=0)
            for r in range(2):
                tile = buffer[x, g * PER : (g + 1) * PER, r].reshape(LANES, length)
                total = tn(stack, tab_ref[r]) + nn(mixer[...], tile)
                tiles[x, g * PER : (g + 1) * PER, r] = total.astype(BF16).reshape(
                    PER, channels, length
                )
        copy_out(x).start()
        return carry

    lax.fori_loop(0, cells, body, 0)
    for x in range(cells):
        copy_out(x).wait()


def cells_call(n, extra, flip, me, src, tab, weight, rows):
    cells, pairs = src.shape[:2]
    out_shape = [jax.ShapeDtypeStruct(src.shape, BF16)]
    if extra:
        out_shape.append(jax.ShapeDtypeStruct(weight.shape, F32))
    return pl.pallas_call(
        functools.partial(cells_kernel, n, extra, flip),
        in_specs=[SMEM, HBM, VMEM, VMEM, VMEM],
        out_specs=[HBM] + [VMEM] * (len(out_shape) - 1),
        out_shape=out_shape,
        scratch_shapes=[
            pltpu.VMEM((pairs // PER * 2, cells * K2, 128), F32),
            pltpu.VMEM((LANES, LANES), BF16),
            pltpu.VMEM(src.shape, BF16),
            pltpu.VMEM(src.shape, BF16),
            pltpu.SemaphoreType.DMA((cells,)),
            pltpu.SemaphoreType.DMA((cells,)),
        ],
        compiler_params=params(56),
        cost_estimate=cost(9e9, 28),
        name="cells",
    )(me, src, tab, weight, rows)


def rows_pointwise_kernel(n, norm, me_ref, field_ref, src_ref, tab_ref, *rest):
    out_ref, grad_ref, hold, square, f_buffer, buffer, f_sems, sems = rest
    outs = messages(out_ref)
    cells, pairs, _, channels, length = src_ref.shape
    copy = fetch(src_ref, buffer, sems)
    f_copy = fetch(field_ref, f_buffer, f_sems)
    square[...] = jnp.zeros(square.shape, F32)

    def body(x, carry):
        copy(x).wait()
        f_copy(x).wait()
        at = pl.ds(pl.multiple_of(x * K2, 8), K2)
        products = square[...]
        for g in range(pairs // PER):
            total = None
            for r in range(2):
                tile = buffer[x, g * PER : (g + 1) * PER, r].reshape(LANES, length)
                left = f_buffer[x, g * PER : (g + 1) * PER, r].reshape(LANES, length)
                products = products + nt(left, tile)
                part = nt(tab_ref[r], tile)
                total = part if total is None else total + part
            hold[2 * g, at, :] = total[:, :128]
            hold[2 * g + 1, at, :] = total[:, 128:]
        square[...] = products
        return carry

    lax.fori_loop(0, cells, body, 0)
    for index, row, k, g in piece_places(me_ref[0], cells, n):
        for r in range(2):
            at = row + r * cells
            for half in range(2):
                outs[index][at : at + cells, half * 128 : (half + 1) * 128] = hold[
                    2 * g + half, pl.ds(k + r * KY, cells, stride=K2), :
                ]
    shape = (LANES, LANES)
    same = iota(shape, 0) // channels == iota(shape, 1) // channels
    diagonal = jnp.where(same, square[...], 0.0)
    fold = (iota((channels, LANES), 1) % channels == iota((channels, LANES), 0)).astype(F32)
    rows = nn_full(fold, diagonal)
    spread = (iota(shape, 0) % channels == iota(shape, 1) % channels).astype(F32)
    full = nn_full(rows, spread)
    keep = iota((channels, LANES), 0) % PER == iota((channels, LANES), 1) // channels
    full = jnp.where(keep, full, 0.0)
    pick = (iota((EXTRA, channels), 1) // PER == iota((EXTRA, channels), 0)).astype(F32)
    grad_ref[...] = nn_full(pick, full) * norm


def rows_pointwise_call(n, norm, me, field, src, tab):
    cells, pairs = src.shape[:2]
    return pl.pallas_call(
        functools.partial(rows_pointwise_kernel, n, norm),
        in_specs=[SMEM, HBM, HBM, VMEM],
        out_specs=[VMEM] * 2,
        out_shape=[message_shape(cells), jax.ShapeDtypeStruct((EXTRA, LANES), F32)],
        scratch_shapes=[
            pltpu.VMEM((pairs // PER * 2, cells * K2, 128), F32),
            pltpu.VMEM((LANES, LANES), F32),
            pltpu.VMEM(src.shape, BF16),
            pltpu.VMEM(src.shape, BF16),
            pltpu.SemaphoreType.DMA((cells,)),
            pltpu.SemaphoreType.DMA((cells,)),
        ],
        compiler_params=params(56),
        cost_estimate=cost(14e9, 34),
        name="rows_pointwise",
    )(me, field, src, tab)


def local_kernels(n, field, cotangent, spectral_weight, local_weight):
    cells = field.shape[0]
    channels = field.shape[3]
    me = lax.axis_index("gx").astype(jnp.int32)[None]

    def permute(array, hop):
        return lax.ppermute(array, "gx", [(i, hop(i)) for i in range(n)])

    planes = [list(range(first, first + NEAR)) for first in range(0, n, NEAR)]

    def near_exchange(rows):
        stacked = rows.reshape(NEAR, rows.shape[0] // NEAR, LANES)
        moved = lax.all_to_all(stacked, "gx", 0, 0, axis_index_groups=planes, tiled=True)
        return moved.reshape(rows.shape)

    def hop(array, s):
        return permute(array, lambda i: far(i, s))

    def far_scatter(parts):
        return [parts[0]] + [hop(parts[s], s) for s in (1, 2, 3)]

    def far_gather(chunk):
        got = hop(chunk, 2)
        return [chunk, hop(chunk, 1), got, hop(got, 1)]

    cos_y, sin_y = np_tables(field.shape[4], KY)
    split_y = np.stack(np.split(complex_rows(cos_y, sin_y), 2, axis=1))
    rows_table = jnp.asarray(split_y.astype(BF16))
    high, low = high_low(split_y)
    cells_table = jnp.asarray(np.concatenate([high, low, high], axis=1))
    def own(table):
        return lax.dynamic_index_in_dim(table, me[0], 0, keepdims=False)

    forward, backward = map(own, x_tables(n, cells))
    lanes = np.arange(channels * channels)
    index = np.arange(channels)[:, None]
    by_c = jnp.asarray((lanes // channels == index).astype(np.float32).astype(BF16))
    by_d = jnp.asarray((lanes % channels == index).astype(np.float32).astype(BF16))
    gather_c = jnp.asarray((lanes // channels == index).astype(np.float32).T.astype(BF16))
    weight = jnp.transpose(spectral_weight, (0, 1, 3, 4, 2))
    norm = 1.0 / math.sqrt(NX * NY * PAIRS * 2.0)

    def after(arrays, *others):
        return lax.optimization_barrier((arrays, others))[0]

    field_out = rows_call(n, me, field, rows_table)
    field_rows = near_exchange(field_out)
    cot_out, grad_part = rows_pointwise_call(
        n, norm, me, after(field, field_out), cotangent, rows_table
    )
    packed = pack_call(after(weight, grad_part))

    field_sums = partial_call(cells, forward, after(field_rows, packed))
    field_parts = far_scatter(field_sums)
    cot_rows = near_exchange(after(cot_out, field_sums))
    mixed, field_hat = mode_call(
        mix_kernel, "mix", channels, packed, [by_c, grad_part], EXTRA, field_parts
    )
    cot_sums = partial_call(cells, forward, after(cot_rows, mixed))
    cot_parts = far_scatter(cot_sums)
    mixed_parts = after(far_gather(mixed), cot_parts)
    mixed_rows = near_exchange(expand_call(cells, backward, mixed_parts))
    back, cot_hat = mode_call(
        adjoint_kernel, "adjoint", channels, packed, [by_d, gather_c], 0, cot_parts
    )
    outer = outer_call(field_hat, after(cot_hat, back))
    grad_spectral = jnp.transpose(outer, (0, 1, 4, 2, 3))
    back_parts = far_gather(back)
    back_rows = near_exchange(expand_call(cells, backward, back_parts))
    output, grad_local = cells_call(
        n, EXTRA, True, me, field, cells_table, local_weight, mixed_rows
    )
    (grad_field,) = cells_call(
        n, 0, False, me, cotangent, cells_table, local_weight, back_rows
    )
    return (output, grad_field, grad_spectral, grad_local)


def solution(mesh):
    n = mesh.shape["gx"]

    def local(field, cotangent, spectral_weight, local_weight):
        tiled = (
            n == 32
            and field.shape == (8, PAIRS, 2, 32, NY)
            and spectral_weight.shape == (2, 32, 32, SLOTS * PER, 24)
        )
        if tiled:
            return local_kernels(n, field, cotangent, spectral_weight, local_weight)
        return local_plain(field, cotangent, spectral_weight, local_weight)

    return jax.shard_map(
        local,
        mesh=mesh,
        in_specs=(
            P(("grp", "gx"), None, None, None, None),
            P(("grp", "gx"), None, None, None, None),
            P(None, None, None, "gx", None),
            P(),
        ),
        out_specs=(
            P(("grp", "gx"), None, None, None, None),
            P(("grp", "gx"), None, None, None, None),
            P(None, None, None, ("grp", "gx"), None),
            P("grp", None),
        ),
        check_vma=False,
    )
```
